256 devices in a mesh: ctx: 64 (over z, x, core), head: 4 (over y).
Axes of the slice: x: 4, y: 4, z: 8, core: 2. Of those that a mesh axis runs over, the one named last changes fastest.
Arguments:
- x_query: bfloat16 [16384, 4096], P('ctx', 'head'), may hold values from -6 to 6
- x_key: bfloat16 [16384, 4096], P('ctx', 'head'), may hold values from -6 to 6
- x_value: bfloat16 [16384, 4096], P('ctx', 'head'), may hold values from -6 to 6
- gate_logits: bfloat16 [16384, 4096], P('ctx', 'head'), may hold values from -6 to 6
- norm_gain: bfloat16 [4096], P('head'), may hold values from 0.099609375 to 1.8984375
- out_grad: bfloat16 [16384, 4096], P('ctx', 'head'), may hold values from -6 to 6
- doc_ids: int32 [16384], P('ctx'), may hold values from 0 to 31, never falling along the last dimension, each value on 1 to 1024 neighbouring positions
Outputs:
- attn_out: bfloat16 [16384, 4096], P('ctx', 'head')
- query_grad: bfloat16 [16384, 4096], P('ctx', 'head')
- key_grad: bfloat16 [16384, 4096], P('ctx', 'head')
- value_grad: bfloat16 [16384, 4096], P('ctx', 'head')
- gate_grad: bfloat16 [16384, 4096], P('ctx', 'head')
- gain_grad: float32 [4096], P('head')
The draws below stay inside these ranges and needn't reach their ends.
Inputs may be any that keep to these rules, and one draw needn't show every extreme that they name: doc_ids never fall along the tokens; each document takes 1 to 1024 consecutive tokens, one exactly 1024.
All inputs are finite; a program needn't handle non-finite values.
Results may differ from the reference program's by a relative error of at most 0.0072.
Values sent between devices are 32-bit elements; how exact they have to be, the bound alone decides.
A program may use at most 128 MiB of HBM per device.

```python
import math
import jax
import jax.numpy as jnp
import numpy as np
from jax import lax

HD = 128
TOK_DEV = 256
HEADS = 32
FEATURES = 4096
TOKENS = 16384
MOST = 1024
DOCS = 32


def block_levels(own_key, shape, split, smallest, top_value):
    factor_of, own = 1.0, jax.random.fold_in(own_key, 6)
    for axis_at, shards_of in split:
        steps = jnp.exp(jax.random.uniform(jax.random.fold_in(own, axis_at), (shards_of,), jnp.float32, smallest / len(split), top_value / len(split)))
        factor_of = factor_of * jnp.repeat(steps, shape[axis_at] // shards_of).reshape([-1 if axis == axis_at else 1 for axis in range(len(shape))])
    return factor_of


def split_up(number_of, total, bound, slope):
    weights = [(1 << 20) // math.isqrt(standing ** slope) + 1 for standing in range(2, number_of + 1)]
    rest, given = total - bound - (number_of - 1), [1] * (number_of - 1)
    while rest > 0:
        free = [i for i in range(number_of - 1) if given[i] < bound]
        whole, budget = sum([weights[i] for i in free]), rest
        for i in free:
            addition = min(bound - given[i], max(1, budget * weights[i] // whole), rest)
            given[i] = given[i] + addition
            rest = rest - addition
    return np.array([bound] + given)


def uneven(rng, amount, total, bound, lean):
    if amount == 2:
        one = jax.random.randint(rng, (), max(1, total - bound), min(bound, total - 1) + 1)
        return jnp.stack([one, total - one])
    tallies = jnp.asarray(split_up(amount, total, bound, lean), jnp.int32)
    couples = (amount - 1) // 2
    donor, taker = tallies[1:1 + 2 * couples:2], tallies[2:2 + 2 * couples:2]
    slack = jnp.minimum(donor - 1, bound - taker)
    passed = jax.random.randint(jax.random.fold_in(rng, 1), (couples,), 0, 1 << 20) % (slack + 1)
    tallies = tallies.at[1:1 + 2 * couples:2].set(donor - passed).at[2:2 + 2 * couples:2].set(taker + passed)
    return tallies[jax.random.permutation(jax.random.fold_in(rng, 2), amount)]


def noise(key, dims, width, bound, pieces=(), kind=jnp.bfloat16):
    result = width * jax.random.normal(key, dims, jnp.float32)
    if pieces:
        result = result * block_levels(key, dims, pieces, -0.22, 0.18)
    return jnp.clip(result, -bound, bound).astype(kind)


def setup_inputs(seed: int = 0) -> dict:
    keys = jax.random.split(jax.random.key(seed), 8)
    x_query = noise(keys[0], (TOKENS, FEATURES), 1.0, 6.0, ((0, 64), (1, 4)))
    x_key = noise(keys[1], (TOKENS, FEATURES), 1.0, 6.0, ((0, 64), (1, 4)))
    x_value = noise(keys[2], (TOKENS, FEATURES), 1.0, 6.0, ((0, 64), (1, 4)))
    gate_logits = noise(keys[3], (TOKENS, FEATURES), 1.0, 6.0, ((0, 64), (1, 4)))
    norm_gain = jnp.clip(1.0 + 0.18 * jax.random.normal(keys[4], (FEATURES,), jnp.float32), 0.099609375, 1.8984375).astype(jnp.bfloat16)
    out_grad = noise(keys[5], (TOKENS, FEATURES), 1.0, 6.0, ((0, 64), (1, 4)))
    doc_ids = jnp.searchsorted(jnp.cumsum(uneven(keys[6], DOCS, TOKENS, MOST, 0)), jnp.arange(TOKENS), side="right").astype(jnp.int32)
    return dict(x_query=x_query, x_key=x_key, x_value=x_value, gate_logits=gate_logits, norm_gain=norm_gain, out_grad=out_grad, doc_ids=doc_ids)


epsilon = 1e-06

def activate(raw):
    wide = raw.astype(jnp.float32)
    return (wide * jax.nn.sigmoid(wide)).astype(jnp.bfloat16)

def silu_slope(raw):
    wide = raw.astype(jnp.float32)
    logistic = jax.nn.sigmoid(wide)
    return logistic * (1.0 + wide * (1.0 - logistic))

def block_mask(labels):
    length = labels.shape[0]
    row_index = lax.broadcasted_iota(jnp.int32, (length, length), 0)
    col_index = lax.broadcasted_iota(jnp.int32, (length, length), 1)
    return (row_index >= col_index) & (labels[:, None] == labels[None, :])

def widen(array):
    return array.astype(jnp.float32)

def reference(x_query, x_key, x_value, gate_logits, norm_gain, out_grad, doc_ids):
    blocks_count = TOKENS // TOK_DEV
    split_shape = (blocks_count, TOK_DEV, HEADS, HD)
    labels_all = doc_ids.reshape(blocks_count, TOK_DEV)
    inputs = (x_query.reshape(split_shape), x_key.reshape(split_shape), x_value.reshape(split_shape), labels_all)

    def forward(running, block_in):
        summed, last_seen = running
        raw_query, raw_key, raw_value, labels = block_in
        query_act = activate(raw_query)
        key_act = activate(raw_key)
        value_act = activate(raw_value)
        allowed = block_mask(labels)
        first_doc = labels[0]
        last_doc = labels[-1]
        scores = jnp.einsum('thd,shd->hts', widen(query_act), widen(key_act))
        weights = jnp.where(allowed[None], scores, 0.0).astype(jnp.bfloat16)
        inside = jnp.einsum('hts,shd->thd', widen(weights), widen(value_act))
        incoming = jnp.where(last_seen == first_doc, summed, jnp.zeros_like(summed))
        rounded_in = incoming.astype(jnp.bfloat16)
        carried_in = jnp.einsum('thd,hde->the', widen(query_act), widen(rounded_in))
        in_first = (labels == first_doc)[:, None, None]
        in_last = (labels == last_doc)[:, None, None]
        mixture = inside + jnp.where(in_first, carried_in, 0.0)
        tail_keys = jnp.where(in_last, widen(key_act), 0.0)
        own_part = jnp.einsum('thd,the->hde', tail_keys, widen(value_act))
        new_sum = own_part + jnp.where(first_doc == last_doc, incoming, jnp.zeros_like(incoming))
        return ((new_sum, last_doc), (mixture, rounded_in))
    neutral = (jnp.zeros((HEADS, HD, HD), jnp.float32), jnp.array(-1, jnp.int32))
    _, (mixture_all, states_all) = lax.scan(forward, neutral, inputs)
    mixture = mixture_all.reshape(TOKENS, HEADS * HD)
    gain_f32 = norm_gain.astype(jnp.float32)
    inv_rms = lax.rsqrt(lax.optimization_barrier(jnp.mean(mixture * mixture, axis=1, keepdims=True)) + epsilon)
    normed = mixture * inv_rms * gain_f32
    gate_open = jax.nn.sigmoid(gate_logits.astype(jnp.float32))
    attn_out = (normed * gate_open).astype(jnp.bfloat16)
    upstream = out_grad.astype(jnp.float32)
    gate_grad = (upstream * normed * gate_open * (1.0 - gate_open)).astype(jnp.bfloat16)
    normed_grad = upstream * gate_open
    gain_grad = lax.optimization_barrier(jnp.sum(normed_grad * mixture * inv_rms, axis=0))
    row_inner = lax.optimization_barrier(jnp.sum(gain_f32 * normed_grad * mixture, axis=1, keepdims=True))
    cubed = inv_rms * inv_rms * inv_rms
    mix_grad = (gain_f32 * normed_grad * inv_rms - mixture * row_inner * cubed / (HEADS * HD)).astype(jnp.bfloat16)
    back_inputs = inputs + (mix_grad.reshape(split_shape), states_all)

    def backward(running, block_in):
        summed, next_first = running
        raw_query, raw_key, raw_value, labels, block_grad, rounded_in = block_in
        query_act = activate(raw_query)
        key_act = activate(raw_key)
        value_act = activate(raw_value)
        allowed = block_mask(labels)
        first_doc = labels[0]
        last_doc = labels[-1]
        in_first = (labels == first_doc)[:, None, None]
        in_last = (labels == last_doc)[:, None, None]
        scores = jnp.einsum('thd,shd->hts', widen(query_act), widen(key_act))
        weights = jnp.where(allowed[None], scores, 0.0).astype(jnp.bfloat16)
        incoming = jnp.where(next_first == last_doc, summed, jnp.zeros_like(summed))
        rounded_grad = incoming.astype(jnp.bfloat16)
        pair_scores = jnp.einsum('thd,shd->hts', widen(block_grad), widen(value_act))
        pair_grad = jnp.where(allowed[None], pair_scores, 0.0).astype(jnp.bfloat16)
        query_part = jnp.einsum('hts,shd->thd', widen(pair_grad), widen(key_act))
        query_part = query_part + jnp.where(in_first, jnp.einsum('the,hde->thd', widen(block_grad), widen(rounded_in)), 0.0)
        key_part = jnp.einsum('hts,thd->shd', widen(pair_grad), widen(query_act))
        key_part = key_part + jnp.where(in_last, jnp.einsum('the,hde->thd', widen(value_act), widen(rounded_grad)), 0.0)
        value_part = jnp.einsum('hts,thd->shd', widen(weights), widen(block_grad))
        value_part = value_part + jnp.where(in_last, jnp.einsum('thd,hde->the', widen(key_act), widen(rounded_grad)), 0.0)
        head_queries = jnp.where(in_first, widen(query_act), 0.0)
        own_part = jnp.einsum('thd,the->hde', head_queries, widen(block_grad))
        new_sum = own_part + jnp.where(first_doc == last_doc, incoming, jnp.zeros_like(incoming))
        grads = ((query_part * silu_slope(raw_query)).astype(jnp.bfloat16), (key_part * silu_slope(raw_key)).astype(jnp.bfloat16), (value_part * silu_slope(raw_value)).astype(jnp.bfloat16))
        return ((new_sum, first_doc), grads)
    _, (query_all, key_all, value_all) = lax.scan(backward, neutral, back_inputs, reverse=True)
    flat = (TOKENS, HEADS * HD)
    return (attn_out, query_all.reshape(flat), key_all.reshape(flat), value_all.reshape(flat), gate_grad, gain_grad)
```

```python
import functools

import jax
import jax.numpy as jnp
from jax import lax
from jax.experimental import pallas as pl
from jax.experimental.pallas import tpu as pltpu
from jax.sharding import PartitionSpec as P

HD = 128
EPS = 1e-06
MESH = pl.DeviceIdType.MESH
F32 = jnp.float32
BF16 = jnp.bfloat16
XS, CORES = 4, 2


def mm(a, b, ca, cb):
    return lax.dot_general(a, b, (((ca,), (cb,)), ((), ())), preferred_element_type=F32)


def sigmoid(x):
    return 0.5 + 0.5 * jnp.tanh(0.5 * x)


def kernel(
    n_ctx, n_head, heads,
    xq_hbm, xk_hbm, xv_hbm, gl_hbm, og_hbm, gain_ref, doc_ref,
    attn_ref, qg_ref, kg_ref, vg_ref, gg_ref, gaing_ref,
    xq, xk, xv, gl, og,
    ka, va, qa, qf, kl, vl, mg,
    wts, mix, ng, gng, sg, kp, vp, sk, sv,
    lab, mask, acc, inv_b, cc_b,
    own, sib_out, sib_in, tsend, tin, st,
    meta, stat, gbuf,
    in_sem, sib_s, sib_r, far_s, far_r, meta_s, meta_r, stat_s, stat_r, gain_s, gain_r,
):
    half = heads // 2
    features = heads * HD * n_head
    c, y = lax.axis_index("ctx"), lax.axis_index("head")
    p = lax.rem(c, 2)
    g = c // 2
    chips = n_ctx // 2
    zs = n_ctx // (XS * CORES)
    z, x = c // (XS * CORES), lax.rem(g, XS)
    sibling = (g * 2 + 1 - p, y)

    def chip(d):
        return (lax.rem(g + d + chips, chips) * 2 + p, y)

    y_peers = [(c, lax.rem(y + d, n_head)) for d in range(1, n_head)]
    x_peers = [((z * XS + lax.rem(x + d, XS)) * 2 + p, y) for d in range(1, XS)]
    z_peers = [((lax.rem(z + d, zs) * XS + x) * 2 + p, y) for d in range(1, zs)]
    near = [chip(1), chip(2), chip(-1), chip(-2)]
    peers = [sibling] + near + y_peers + x_peers + z_peers

    loads = []
    for i, (src, dst) in enumerate(((xk_hbm, xk), (xv_hbm, xv), (xq_hbm, xq), (gl_hbm, gl), (og_hbm, og))):
        cp = pltpu.make_async_copy(src, dst, in_sem.at[i])
        cp.start()
        loads.append(cp)
    barrier = pltpu.get_barrier_semaphore()
    for q in peers:
        pl.semaphore_signal(barrier, inc=1, device_id=q, device_id_type=MESH)

    def remote(src, dst, ssem, rsem, dev):
        return pltpu.make_async_remote_copy(
            src_ref=src, dst_ref=dst, send_sem=ssem, recv_sem=rsem, device_id=dev, device_id_type=MESH
        )

    def loop(n, body):
        lax.fori_loop(0, n, lambda i, carry: (body(i), carry)[1], 0)

    def cols(h):
        return pl.ds(pl.multiple_of(h * HD, HD), HD)

    row = doc_ref[...].astype(F32)
    tokens = row.shape[1]
    lab[...] = jnp.broadcast_to(row, (HD, tokens)).T
    first, last = lab[0:1, :], lab[tokens - 1 : tokens, :]
    meta[0] = jnp.zeros(meta.shape[1:], F32)
    meta[2] = jnp.zeros(meta.shape[1:], F32)
    stat[0] = jnp.zeros(stat.shape[1:], F32)
    meta[0, 0:1, :] = first
    meta[0, 1:2, :] = last

    def own_part(h):
        s = cols(h)
        k = xk[:, s].astype(F32)
        v = xv[:, s].astype(F32)
        kb = (k * sigmoid(k)).astype(BF16)
        vb = (v * sigmoid(v)).astype(BF16)
        ka[:, s] = kb
        va[:, s] = vb
        in_last = lab[...] == lab[tokens - 1 : tokens, :]
        kb = jnp.where(in_last, kb.astype(F32), 0.0).astype(BF16)
        kl[:, s] = kb
        own[h] = mm(kb, vb, 0, 0)

    def sib_copy(d, i, src):
        return remote(src, sib_in.at[d, i], sib_s.at[d, i], sib_r.at[d, i], sibling)

    def far_copy(d, i, k):
        step = (k + 1) * (1 if d == 0 else -1)
        return remote(tsend.at[d, i], tin.at[d, k, i], far_s.at[d, k, i], far_r.at[d, k, i], chip(step))

    def meta_copy(k):
        if k == 0:
            return remote(meta.at[0], meta.at[1], meta_s.at[0], meta_r.at[0], sibling)
        return remote(meta.at[2], meta.at[2 + k], meta_s.at[k], meta_r.at[k], near[k - 1])

    loads[0].wait()
    loads[1].wait()
    mine = p * half
    other = (1 - p) * half
    own_part(other)
    pl.semaphore_wait(barrier, len(peers))
    meta_copy(0).start()
    sib_copy(0, 0, own.at[other]).start()

    def send_own(i):
        own_part(other + i + 1)
        sib_copy(0, i + 1, own.at[other + i + 1]).start()

    loop(half - 1, send_own)

    own_part(mine)
    meta_copy(0).wait_recv()
    lo = p == 0
    f_lo = jnp.where(lo, meta[0, 0:1, :], meta[1, 0:1, :])
    l_lo = jnp.where(lo, meta[0, 1:2, :], meta[1, 1:2, :])
    f_hi = jnp.where(lo, meta[1, 0:1, :], meta[0, 0:1, :])
    l_hi = jnp.where(lo, meta[1, 1:2, :], meta[0, 1:2, :])
    meta[2, 0:1, :] = f_lo
    meta[2, 1:2, :] = l_hi
    for k in range(1, 5):
        meta_copy(k).start()

    def send_total(i, d):
        a, b = own[mine + i], sib_in[d, i]
        lo_part, hi_part = jnp.where(lo, a, b), jnp.where(lo, b, a)
        if d == 0:
            total = hi_part + jnp.where(l_lo == l_hi, lo_part, 0.0)
        else:
            total = lo_part + jnp.where(f_lo == f_hi, hi_part, 0.0)
        tsend[d, i] = total
        far_copy(d, i, 0).start()
        far_copy(d, i, 1).start()

    def fwd_total(i):
        @pl.when(i > 0)
        def _():
            own_part(mine + i)

        sib_copy(0, i, own.at[other + i]).wait_recv()
        send_total(i, 0)

    loop(half, fwd_total)

    t_iota = lax.broadcasted_iota(jnp.int32, (tokens, tokens), 0)
    s_iota = lax.broadcasted_iota(jnp.int32, (tokens, tokens), 1)
    lab2 = jnp.concatenate([lab[...]] * (tokens // HD), axis=1)
    mask[...] = jnp.where((lab2 == row) & (t_iota >= s_iota), 1.0, 0.0)
    loads[2].wait()
    loads[3].wait()
    loads[4].wait()

    def inside(h):
        s = cols(h)
        q = xq[:, s].astype(F32)
        qb = (q * sigmoid(q)).astype(BF16)
        qa[:, s] = qb
        in_first = lab[...] == lab[0:1, :]
        qf[:, s] = jnp.where(in_first, qb.astype(F32), 0.0).astype(BF16)
        w = (mm(qb, ka[:, s], 1, 1) * mask[...]).astype(BF16)
        wts[h] = w
        mix[:, s] = mm(w, va[:, s], 1, 0)
        gate = sigmoid(gl[:, s].astype(F32))
        sg[:, s] = gate
        grad = og[:, s].astype(F32) * gate
        ng[:, s] = grad
        gng[:, s] = grad * gain_ref[:, s].astype(F32)
        v = xv[:, s].astype(F32)
        gv = sigmoid(v)
        sv[:, s] = gv * (1.0 + v * (1.0 - gv))
        k = xk[:, s].astype(F32)
        gk = sigmoid(k)
        sk[:, s] = gk * (1.0 + k * (1.0 - gk))
        in_last = lab[...] == lab[tokens - 1 : tokens, :]
        vl[:, s] = jnp.where(in_last, va[:, s].astype(F32), 0.0).astype(BF16)

    loop(heads, inside)
    acc[...] = jnp.zeros_like(acc)

    for k in range(1, 5):
        meta_copy(k).wait_recv()

    def receive(d, i, finish):
        far_copy(d, i, 0).wait_recv()
        far_copy(d, i, 1).wait_recv()
        a, b = own[mine + i], sib_in[d, i]
        lo_part, hi_part = jnp.where(lo, a, b), jnp.where(lo, b, a)
        if d == 0:
            near_ok, far_ok = meta[3, 1:2, :] == f_lo, meta[4, 1:2, :] == f_lo
            edge = jnp.where(near_ok, tin[d, 0, i], 0.0) + jnp.where(far_ok, tin[d, 1, i], 0.0)
            inner = jnp.where(l_lo == f_hi, lo_part, 0.0) + jnp.where(f_lo == f_hi, edge, 0.0)
            to_lo, to_hi = edge, inner
        else:
            near_ok, far_ok = meta[5, 0:1, :] == l_hi, meta[6, 0:1, :] == l_hi
            edge = jnp.where(near_ok, tin[d, 0, i], 0.0) + jnp.where(far_ok, tin[d, 1, i], 0.0)
            inner = jnp.where(f_hi == l_lo, hi_part, 0.0) + jnp.where(l_hi == l_lo, edge, 0.0)
            to_lo, to_hi = inner, edge
        sib_out[d, i] = jnp.where(lo, to_hi, to_lo)
        sib_copy(d, half + i, sib_out.at[d, i]).start()
        st[d, mine + i] = jnp.where(lo, to_lo, to_hi).astype(BF16)
        finish(mine + i)

    def receive_sib(d, i, finish):
        sib_copy(d, half + i, sib_out.at[d, i]).wait_recv()
        st[d, other + i] = sib_in[d, half + i].astype(BF16)
        finish(other + i)

    def mixture(h):
        s = cols(h)
        m = mix[:, s] + mm(qf[:, s], st[0, h], 1, 0)
        mix[:, s] = m
        acc[0] += m * m
        acc[1] += gng[:, s] * m

    loop(half, lambda i: receive(0, i, mixture))
    loop(half, lambda i: receive_sib(0, i, mixture))

    stat[0, 0:1, :] = jnp.sum(acc[0].T, axis=0, keepdims=True)
    stat[0, 1:2, :] = jnp.sum(acc[1].T, axis=0, keepdims=True)

    def stat_copy(k):
        return remote(stat.at[0], stat.at[1 + k], stat_s.at[k], stat_r.at[k], y_peers[k])

    for k in range(n_head - 1):
        stat_copy(k).start()
    for k in range(n_head - 1):
        stat_copy(k).wait_recv()
    rows = stat[0]
    for k in range(n_head - 1):
        rows = rows + stat[1 + k]
    inv = lax.rsqrt(rows[0:1, :] / features + EPS)
    cc = rows[1:2, :] * (inv * inv * inv) / features
    inv_b[...] = jnp.broadcast_to(inv, (HD, tokens)).T
    cc_b[...] = jnp.broadcast_to(cc, (HD, tokens)).T

    def grad_part(h):
        s = cols(h)
        m = (gng[:, s] * inv_b[...] - mix[:, s] * cc_b[...]).astype(BF16)
        mg[:, s] = m
        own[h] = mm(qf[:, s], m, 0, 0)

    for i in range(half):
        sib_copy(0, i, own.at[other + i]).wait_send()

    def send_grad(i):
        grad_part(other + i)
        sib_copy(1, i, own.at[other + i]).start()

    loop(half, send_grad)

    def bwd_total(i):
        grad_part(mine + i)
        sib_copy(1, i, own.at[other + i]).wait_recv()
        send_total(i, 1)

    loop(half, bwd_total)

    def tail(h):
        s = cols(h)
        unit = mix[:, s] * inv_b[...]
        gbuf[0, pl.ds(h, 1), :] = jnp.sum(ng[:, s] * unit, axis=0, keepdims=True)
        normed = unit * gain_ref[:, s].astype(F32)
        gate = sg[:, s]
        attn_ref[:, s] = (normed * gate).astype(BF16)
        gg_ref[:, s] = (ng[:, s] * normed * (1.0 - gate)).astype(BF16)

    loop(heads, tail)

    def gain_copy(slot, dst, k, dev):
        return remote(gbuf.at[slot], gbuf.at[dst], gain_s.at[k], gain_r.at[k], dev)

    core_copy = gain_copy(0, 3, 0, sibling)
    x_copies = [gain_copy(1, 4 + k, 1 + k, q) for k, q in enumerate(x_peers)]
    z_copies = [gain_copy(2, 4 + XS - 1 + k, XS + k, q) for k, q in enumerate(z_peers)]
    core_copy.start()

    def pair(h):
        s = cols(h)
        m = mg[:, s]
        w = wts[h]
        pg = (mm(m, va[:, s], 1, 1) * mask[...]).astype(BF16)
        vp[:, s] = mm(w, m, 0, 0)
        kp[:, s] = mm(pg, qa[:, s], 0, 0)
        q = xq[:, s].astype(F32)
        gq = sigmoid(q)
        slope = gq * (1.0 + q * (1.0 - gq))
        in_first = lab[...] == lab[0:1, :]
        part = mm(pg, ka[:, s], 1, 0) + jnp.where(in_first, mm(m, st[0, h], 1, 1), 0.0)
        qg_ref[:, s] = (part * slope).astype(BF16)

    pair(0)
    core_copy.wait_recv()
    gbuf[1] = gbuf[0] + gbuf[3]
    for cp in x_copies:
        cp.start()
    loop(half - 1, lambda i: pair(i + 1))
    total = gbuf[1]
    for k, cp in enumerate(x_copies):
        cp.wait_recv()
        total = total + gbuf[4 + k]
    gbuf[2] = total
    for cp in z_copies:
        cp.start()
    loop(half, lambda i: pair(half + i))

    def final(h):
        s = cols(h)
        gb = st[1, h]
        kg_ref[:, s] = ((kp[:, s] + mm(vl[:, s], gb, 1, 1)) * sk[:, s]).astype(BF16)
        vg_ref[:, s] = ((vp[:, s] + mm(kl[:, s], gb, 1, 0)) * sv[:, s]).astype(BF16)

    loop(half, lambda i: receive(1, i, final))
    total = gbuf[2]
    for k, cp in enumerate(z_copies):
        cp.wait_recv()
        total = total + gbuf[4 + XS - 1 + k]
    gaing_ref[...] = total
    loop(half, lambda i: receive_sib(1, i, final))

    for k in range(5):
        meta_copy(k).wait_send()
    for k in range(n_head - 1):
        stat_copy(k).wait_send()
    for cp in [core_copy] + x_copies + z_copies:
        cp.wait_send()

    def drain(i):
        sib_copy(1, i, own.at[other + i]).wait_send()
        for d in (0, 1):
            sib_copy(d, half + i, sib_out.at[d, i]).wait_send()
            far_copy(d, i, 0).wait_send()
            far_copy(d, i, 1).wait_send()

    loop(half, drain)


def local(n_ctx, n_head, x_query, x_key, x_value, gate_logits, norm_gain, out_grad, doc_ids):
    tokens, width = x_query.shape
    heads = width // HD
    half = heads // 2
    zs = n_ctx // (XS * CORES)
    flat16 = pltpu.VMEM((tokens, width), BF16)
    flat32 = pltpu.VMEM((tokens, width), F32)
    square = pltpu.VMEM((tokens, tokens), F32)
    thin = pltpu.VMEM((tokens, HD), F32)
    state = lambda *lead: pltpu.VMEM((*lead, HD, HD), F32)
    dma = pltpu.SemaphoreType.DMA
    n_gain = 1 + (XS - 1) + (zs - 1)
    vmem = pl.BlockSpec(memory_space=pltpu.VMEM)
    anywhere = pl.BlockSpec(memory_space=pl.ANY)
    big = jax.ShapeDtypeStruct((tokens, width), BF16)
    outs = pl.pallas_call(
        functools.partial(kernel, n_ctx, n_head, heads),
        out_shape=(big, big, big, big, big, jax.ShapeDtypeStruct((heads, HD), F32)),
        in_specs=[anywhere] * 5 + [vmem] * 2,
        out_specs=(vmem,) * 6,
        scratch_shapes=[flat16] * 5 + [flat16] * 7
        + [pltpu.VMEM((heads, tokens, tokens), BF16)] + [flat32] * 8
        + [thin, square, pltpu.VMEM((2, tokens, HD), F32), thin, thin]
        + [
            state(heads), state(2, half), state(2, 2 * half), state(2, half), state(2, 2, half),
            pltpu.VMEM((2, heads, HD, HD), BF16),
            pltpu.VMEM((7, 8, HD), F32),
            pltpu.VMEM((n_head, 8, tokens), F32),
            pltpu.VMEM((3 + n_gain, heads, HD), F32),
            dma((5,)), dma((2, 2 * half)), dma((2, 2 * half)), dma((2, 2, half)), dma((2, 2, half)),
            dma((5,)), dma((5,)), dma((n_head - 1,)), dma((n_head - 1,)), dma((n_gain,)), dma((n_gain,)),
        ],
        compiler_params=pltpu.CompilerParams(
            collective_id=0, has_side_effects=True, vmem_limit_bytes=56 << 20
        ),
        cost_estimate=pl.CostEstimate(flops=1 << 30, bytes_accessed=5 << 20, transcendentals=1 << 20),
    )(x_query, x_key, x_value, gate_logits, out_grad, norm_gain.reshape(1, width), doc_ids.reshape(1, tokens))
    return (*outs[:5], outs[5].reshape(width))


def solution(mesh):
    n_ctx, n_head = mesh.shape["ctx"], mesh.shape["head"]
    placed = (
        P("ctx", "head"), P("ctx", "head"), P("ctx", "head"), P("ctx", "head"),
        P("head"), P("ctx", "head"), P("ctx"),
    )
    return jax.shard_map(
        functools.partial(local, n_ctx, n_head),
        mesh=mesh,
        in_specs=placed,
        out_specs=(P("ctx", "head"),) * 5 + (P("head"),),
        check_vma=False,
    )
```

```python
import functools

import jax
import jax.numpy as jnp
from jax import lax
from jax.experimental import pallas as pl
from jax.experimental.pallas import tpu as pltpu
from jax.sharding import PartitionSpec as P

HD = 128
EPS = 1e-06
MESH = pl.DeviceIdType.MESH
F32 = jnp.float32
BF16 = jnp.bfloat16
XS, CORES = 4, 2
VIA_NEXT = 1


def mm(a, b, ca, cb):
    return lax.dot_general(a, b, (((ca,), (cb,)), ((), ())), preferred_element_type=F32)


def sigmoid(x):
    return 0.5 + 0.5 * jnp.tanh(0.5 * x)


def kernel(
    n_ctx, n_head, heads,
    xq_hbm, xk_hbm, xv_hbm, gl_hbm, og_hbm, gain_ref, doc_ref,
    attn_ref, qg_ref, kg_ref, vg_ref, gg_ref, gaing_ref,
    xq, xk, xv, gl, og,
    ka, va, qa, qf, kl, vl, mg,
    wts, mix, ng, gng, sg, kp, vp, sk, sv,
    gain8, lab, mask, acc, inv_b, cc_b,
    own, sib_out, sib_in, tsend, tin, rx, st,
    meta, stat, gbuf,
    in_sem, sib_s, sib_r, far_s, far_r, meta_s, meta_r, stat_s, stat_r, gain_s, gain_r, rel_s, rel_r, token,
):
    half = heads // 2
    features = heads * HD * n_head
    c, y = lax.axis_index("ctx"), lax.axis_index("head")
    p = lax.rem(c, 2)
    g = c // 2
    chips = n_ctx // 2
    zs = n_ctx // (XS * CORES)
    z, x = c // (XS * CORES), lax.rem(g, XS)
    sibling = (g * 2 + 1 - p, y)

    def chip(d):
        return ((g + d) * 2 + p, y)

    def exists(chip_index):
        return (chip_index >= 0) & (chip_index < chips)

    def in_row(d):
        return z * XS + lax.rem(x + d + XS, XS)

    def at_z(other_z):
        return ((other_z * XS + x) * 2 + p, y)

    def when(cond, act):
        pl.when(cond)(act)

    y_peers = [(c, lax.rem(y + d, n_head)) for d in range(1, n_head)]
    row_peers = [(in_row(d) * 2 + q, y) for d in range(1, XS) for q in (p, 1 - p)]
    quad = min(zs, 4)
    quad_peers = [at_z(z // quad * quad + lax.rem(z + d, quad)) for d in range(1, quad)]
    far_z = lax.rem(z + quad, zs)
    bridge = (z >= 2) & (z < 6)
    near = [chip(k) for k in (1, 2, -1, -2)]
    near_ok = [exists(g + k) for k in (1, 2, -1, -2)]
    always = [sibling] + y_peers + row_peers[1::2] + quad_peers
    chain = [(chip(k), exists(g + k)) for k in (1, 2, 3, -1, -2, -3)]
    across = at_z(jnp.where(z < quad, z + 2, z - 2))

    loads = []
    for i, (src, dst) in enumerate(((xk_hbm, xk), (xv_hbm, xv), (xq_hbm, xq), (gl_hbm, gl), (og_hbm, og))):
        cp = pltpu.make_async_copy(src, dst, in_sem.at[i])
        cp.start()
        loads.append(cp)
    barrier = pltpu.get_barrier_semaphore()
    greeted = jnp.int32(len(always))
    for q in always:
        pl.semaphore_signal(barrier, inc=1, device_id=q, device_id_type=MESH)
    for q, there in chain + ([(across, bridge)] if zs > quad else []):
        when(there, lambda q=q: pl.semaphore_signal(barrier, inc=1, device_id=q, device_id_type=MESH))
        greeted = greeted + there.astype(jnp.int32)

    def remote(src, dst, ssem, rsem, dev):
        return pltpu.make_async_remote_copy(
            src_ref=src, dst_ref=dst, send_sem=ssem, recv_sem=rsem, device_id=dev, device_id_type=MESH
        )

    def loop(n, body):
        lax.fori_loop(0, n, lambda i, carry: (body(i), carry)[1], 0)

    def cols(h):
        return pl.ds(pl.multiple_of(h * HD, HD), HD)

    row = doc_ref[...].astype(F32)
    tokens = row.shape[1]
    lab[...] = jnp.broadcast_to(row, (HD, tokens)).T
    first, last = lab[0:1, :], lab[tokens - 1 : tokens, :]
    meta[0] = jnp.zeros(meta.shape[1:], F32)
    meta[2] = jnp.zeros(meta.shape[1:], F32)
    stat[0] = jnp.zeros(stat.shape[1:], F32)
    meta[0, 0:1, :] = first
    meta[0, 1:2, :] = last

    def own_part(h):
        s = cols(h)
        k = xk[:, s].astype(F32)
        v = xv[:, s].astype(F32)
        kb = (k * sigmoid(k)).astype(BF16)
        vb = (v * sigmoid(v)).astype(BF16)
        ka[:, s] = kb
        va[:, s] = vb
        in_last = lab[...] == lab[tokens - 1 : tokens, :]
        kb = jnp.where(in_last, kb.astype(F32), 0.0).astype(BF16)
        kl[:, s] = kb
        own[h] = mm(kb, vb, 0, 0)

    def sib_copy(d, i, src):
        return remote(src, sib_in.at[d, i], sib_s.at[d, i], sib_r.at[d, i], sibling)

    def ok(d, k):
        return exists(g + k * (1 - 2 * d))

    def next_copy(d, i):
        return remote(tsend.at[d, i], tin.at[d, 0, i], far_s.at[d, 0, i], far_r.at[d, 0, i], chip(1 - 2 * d))

    def pass_copy(d, i):
        return remote(tin.at[d, 0, i], tin.at[d, 1, i], far_s.at[d, 1, i], far_r.at[d, 1, i], chip(1 - 2 * d))

    def back_copy(d, i):
        return remote(tsend.at[d, i], rx.at[d, i], rel_s.at[d, i], rel_r.at[d, i], (in_row(2 * d - 1) * 2 + p, y))

    def relay_target(d):
        return in_row(1 - 2 * d) + 2 * (1 - 2 * d)

    def relay_copy(d, i):
        return remote(rx.at[d, i], tin.at[d, 1, i], far_s.at[d, 1, i], far_r.at[d, 1, i], (relay_target(d) * 2 + p, y))

    def pass_on(d, i):
        when(ok(d, -1), lambda: next_copy(d, i).wait_recv())
        when(ok(d, -1) & ok(d, 1), lambda: pass_copy(d, i).start())

    def relay(d, i):
        def act():
            back_copy(d, i).wait_recv()
            relay_copy(d, i).start()

        when(exists(relay_target(d)), act)

    def meta_copy(k):
        if k == 0:
            return remote(meta.at[0], meta.at[1], meta_s.at[0], meta_r.at[0], sibling)
        return remote(meta.at[2], meta.at[2 + k], meta_s.at[k], meta_r.at[k], near[k - 1])

    loads[0].wait()
    loads[1].wait()
    mine = p * half
    other = (1 - p) * half
    own_part(other)
    pl.semaphore_wait(barrier, greeted)
    if zs > quad:
        def tell():
            for dz in (-2, 2):
                pl.semaphore_signal(token, inc=1, device_id=at_z(z + dz), device_id_type=MESH)

        when(bridge, tell)
    meta_copy(0).start()
    sib_copy(0, 0, own.at[other]).start()

    def send_own(i):
        own_part(other + i + 1)
        sib_copy(0, i + 1, own.at[other + i + 1]).start()

    loop(half - 1, send_own)

    own_part(mine)
    meta_copy(0).wait_recv()
    lo = p == 0
    f_lo = jnp.where(lo, meta[0, 0:1, :], meta[1, 0:1, :])
    l_lo = jnp.where(lo, meta[0, 1:2, :], meta[1, 1:2, :])
    f_hi = jnp.where(lo, meta[1, 0:1, :], meta[0, 0:1, :])
    l_hi = jnp.where(lo, meta[1, 1:2, :], meta[0, 1:2, :])
    meta[2, 0:1, :] = f_lo
    meta[2, 1:2, :] = l_hi
    for k in range(1, 5):
        when(near_ok[k - 1], lambda k=k: meta_copy(k).start())

    def send_total(i, d):
        a, b = own[mine + i], sib_in[d, i]
        lo_part, hi_part = jnp.where(lo, a, b), jnp.where(lo, b, a)
        if d == 0:
            total = hi_part + jnp.where(l_lo == l_hi, lo_part, 0.0)
        else:
            total = lo_part + jnp.where(f_lo == f_hi, hi_part, 0.0)
        tsend[d, i] = total
        when(ok(d, 1), lambda: next_copy(d, i).start())
        when(ok(d, 2) & (i >= VIA_NEXT), lambda: back_copy(d, i).start())

    def fwd_total(i):
        @pl.when(i > 0)
        def _():
            own_part(mine + i)

        sib_copy(0, i, own.at[other + i]).wait_recv()
        send_total(i, 0)

    loop(half, fwd_total)

    t_iota = lax.broadcasted_iota(jnp.int32, (tokens, tokens), 0)
    s_iota = lax.broadcasted_iota(jnp.int32, (tokens, tokens), 1)
    lab2 = jnp.concatenate([lab[...]] * (tokens // HD), axis=1)
    mask[...] = jnp.where((lab2 == row) & (t_iota >= s_iota), 1.0, 0.0)
    gain8[...] = gain_ref[...].astype(F32).reshape(heads, HD)
    loads[2].wait()
    loads[3].wait()
    loads[4].wait()

    def inside(h):
        s = cols(h)
        q = xq[:, s].astype(F32)
        qb = (q * sigmoid(q)).astype(BF16)
        qa[:, s] = qb
        in_first = lab[...] == lab[0:1, :]
        qf[:, s] = jnp.where(in_first, qb.astype(F32), 0.0).astype(BF16)
        w = (mm(qb, ka[:, s], 1, 1) * mask[...]).astype(BF16)
        wts[h] = w
        mix[:, s] = mm(w, va[:, s], 1, 0)
        gate = sigmoid(gl[:, s].astype(F32))
        sg[:, s] = gate
        grad = og[:, s].astype(F32) * gate
        ng[:, s] = grad
        gng[:, s] = grad * gain8[pl.ds(h, 1), :]
        v = xv[:, s].astype(F32)
        gv = sigmoid(v)
        sv[:, s] = gv * (1.0 + v * (1.0 - gv))
        k = xk[:, s].astype(F32)
        gk = sigmoid(k)
        sk[:, s] = gk * (1.0 + k * (1.0 - gk))
        in_last = lab[...] == lab[tokens - 1 : tokens, :]
        vl[:, s] = jnp.where(in_last, va[:, s].astype(F32), 0.0).astype(BF16)

    turns = [lambda i=i: pass_on(0, i) for i in range(VIA_NEXT)] + [lambda i=i: relay(0, i) for i in range(VIA_NEXT, half)]
    split = heads - half // 2 - 1
    loop(split, inside)
    for j in range(half):
        turns[j]()
        if split + j < heads:
            inside(split + j)
    acc[...] = jnp.zeros_like(acc)

    for k, (back, slot) in enumerate(((2, 3), (3, 4), (0, 5), (1, 6))):
        when(near_ok[back], lambda k=k: meta_copy(k + 1).wait_recv())

        def missing(slot=slot):
            meta[slot] = jnp.full(meta.shape[1:], -1.0, F32)

        when(jnp.logical_not(near_ok[back]), missing)

    def receive(d, i, finish):
        when(ok(d, -1) & (i >= VIA_NEXT), lambda: next_copy(d, i).wait_recv())
        when(ok(d, -2), lambda: relay_copy(d, i).wait_recv())
        a, b = own[mine + i], sib_in[d, i]
        lo_part, hi_part = jnp.where(lo, a, b), jnp.where(lo, b, a)
        if d == 0:
            one, two = meta[3, 1:2, :] == f_lo, meta[4, 1:2, :] == f_lo
            edge = jnp.where(one, tin[d, 0, i], 0.0) + jnp.where(two, tin[d, 1, i], 0.0)
            inner = jnp.where(l_lo == f_hi, lo_part, 0.0) + jnp.where(f_lo == f_hi, edge, 0.0)
            to_lo, to_hi = edge, inner
        else:
            one, two = meta[5, 0:1, :] == l_hi, meta[6, 0:1, :] == l_hi
            edge = jnp.where(one, tin[d, 0, i], 0.0) + jnp.where(two, tin[d, 1, i], 0.0)
            inner = jnp.where(f_hi == l_lo, hi_part, 0.0) + jnp.where(l_hi == l_lo, edge, 0.0)
            to_lo, to_hi = inner, edge
        sib_out[d, i] = jnp.where(lo, to_hi, to_lo)
        sib_copy(d, half + i, sib_out.at[d, i]).start()
        st[d, mine + i] = jnp.where(lo, to_lo, to_hi).astype(BF16)
        finish(mine + i)

    def receive_sib(d, i, finish):
        sib_copy(d, half + i, sib_out.at[d, i]).wait_recv()
        st[d, other + i] = sib_in[d, half + i].astype(BF16)
        finish(other + i)

    def mixture(h):
        s = cols(h)
        m = mix[:, s] + mm(qf[:, s], st[0, h], 1, 0)
        mix[:, s] = m
        acc[0] += m * m
        acc[1] += gng[:, s] * m

    loop(half, lambda i: receive(0, i, mixture))
    loop(half, lambda i: receive_sib(0, i, mixture))

    stat[0, 0:1, :] = jnp.sum(acc[0].T, axis=0, keepdims=True)
    stat[0, 1:2, :] = jnp.sum(acc[1].T, axis=0, keepdims=True)

    def stat_copy(k):
        return remote(stat.at[0], stat.at[1 + k], stat_s.at[k], stat_r.at[k], y_peers[k])

    for k in range(n_head - 1):
        stat_copy(k).start()
    for k in range(n_head - 1):
        stat_copy(k).wait_recv()
    rows = stat[0]
    for k in range(n_head - 1):
        rows = rows + stat[1 + k]
    inv = lax.rsqrt(rows[0:1, :] / features + EPS)
    cc = rows[1:2, :] * (inv * inv * inv) / features
    inv_b[...] = jnp.broadcast_to(inv, (HD, tokens)).T
    cc_b[...] = jnp.broadcast_to(cc, (HD, tokens)).T

    def grad_part(h):
        s = cols(h)
        inv_r = inv_b[...]
        plain = mix[:, s]
        gbuf[0, pl.ds(h, 1), :] = jnp.sum(ng[:, s] * plain * inv_r, axis=0, keepdims=True)
        m = (gng[:, s] * inv_r - plain * cc_b[...]).astype(BF16)
        mg[:, s] = m
        own[h] = mm(qf[:, s], m, 0, 0)

    for i in range(half):
        sib_copy(0, i, own.at[other + i]).wait_send()

    def send_grad(i):
        grad_part(other + i)
        sib_copy(1, i, own.at[other + i]).start()

    loop(half, send_grad)

    def bwd_total(i):
        grad_part(mine + i)
        sib_copy(1, i, own.at[other + i]).wait_recv()
        send_total(i, 1)

    loop(half, bwd_total)

    def gain_copy(slot, dst, k, dev):
        return remote(gbuf.at[slot], gbuf.at[dst], gain_s.at[k], gain_r.at[k], dev)

    stages, k = [], 0
    for partners in ([sibling] + row_peers, quad_peers, [at_z(far_z)] if zs > quad else []):
        stages.append([gain_copy(len(stages), 4 + k + j, k + j, q) for j, q in enumerate(partners)])
        k += len(partners)

    def gain_stage(n):
        total, first_slot = gbuf[n], 4 + sum(len(st_) for st_ in stages[:n])
        for j, cp in enumerate(stages[n]):
            cp.wait_recv()
            total = total + gbuf[first_slot + j]
        if n == 2:
            gaing_ref[...] = total
            return
        gbuf[n + 1] = total
        if n == 1 and zs > quad:
            pl.semaphore_wait(token, 1)
        for cp in stages[n + 1]:
            cp.start()

    for cp in stages[0]:
        cp.start()

    def tail(h):
        s = cols(h)
        normed = mix[:, s] * inv_b[...] * gain8[pl.ds(h, 1), :]
        gate = sg[:, s]
        attn_ref[:, s] = (normed * gate).astype(BF16)
        gg_ref[:, s] = (ng[:, s] * normed * (1.0 - gate)).astype(BF16)

    loop(heads, tail)

    def pair(h):
        s = cols(h)
        m = mg[:, s]
        w = wts[h]
        pg = (mm(m, va[:, s], 1, 1) * mask[...]).astype(BF16)
        vp[:, s] = mm(w, m, 0, 0)
        kp[:, s] = mm(pg, qa[:, s], 0, 0)
        q = xq[:, s].astype(F32)
        gq = sigmoid(q)
        slope = gq * (1.0 + q * (1.0 - gq))
        in_first = lab[...] == lab[0:1, :]
        part = mm(pg, ka[:, s], 1, 0) + jnp.where(in_first, mm(m, st[0, h], 1, 1), 0.0)
        qg_ref[:, s] = (part * slope).astype(BF16)

    turns = [lambda i=i: pass_on(1, i) for i in range(VIA_NEXT)] + [lambda i=i: relay(1, i) for i in range(VIA_NEXT, half)]
    loop(half, pair)
    turns[0]()
    gain_stage(0)
    for j in range(1, half):
        pair(half + j - 1)
        turns[j]()
    pair(heads - 1)
    gain_stage(1)

    def final(h):
        s = cols(h)
        gb = st[1, h]
        kg_ref[:, s] = ((kp[:, s] + mm(vl[:, s], gb, 1, 1)) * sk[:, s]).astype(BF16)
        vg_ref[:, s] = ((vp[:, s] + mm(kl[:, s], gb, 1, 0)) * sv[:, s]).astype(BF16)

    loop(half, lambda i: receive(1, i, final))
    loop(half, lambda i: receive_sib(1, i, final))
    gain_stage(2)

    meta_copy(0).wait_send()
    for k in range(1, 5):
        when(near_ok[k - 1], lambda k=k: meta_copy(k).wait_send())
    for k in range(n_head - 1):
        stat_copy(k).wait_send()
    for stage in stages:
        for cp in stage:
            cp.wait_send()

    def drain(i):
        sib_copy(1, i, own.at[other + i]).wait_send()
        for d in (0, 1):
            sib_copy(d, half + i, sib_out.at[d, i]).wait_send()
            when(ok(d, 1), lambda d=d: next_copy(d, i).wait_send())
            when(ok(d, 1) & ok(d, -1) & (i < VIA_NEXT), lambda d=d: pass_copy(d, i).wait_send())

            def relayed(d=d):
                relay_copy(d, i).wait_send()

            when(ok(d, 2) & (i >= VIA_NEXT), lambda d=d: back_copy(d, i).wait_send())
            when(exists(relay_target(d)) & (i >= VIA_NEXT), relayed)

    loop(half, drain)


def write_kernel(n, *refs):
    sems = refs[-1]
    copies = [pltpu.make_async_copy(refs[i], refs[n + i], sems.at[i]) for i in range(n)]
    for cp in copies:
        cp.start()
    for cp in copies:
        cp.wait()


def write_out(arrays):
    n = len(arrays)
    return pl.pallas_call(
        functools.partial(write_kernel, n),
        out_shape=tuple(jax.ShapeDtypeStruct(a.shape, a.dtype) for a in arrays),
        in_specs=[pl.BlockSpec(memory_space=pltpu.VMEM)] * n,
        out_specs=(pl.BlockSpec(memory_space=pl.ANY),) * n,
        scratch_shapes=[pltpu.SemaphoreType.DMA((n,))],
    )(*arrays)


def local(n_ctx, n_head, x_query, x_key, x_value, gate_logits, norm_gain, out_grad, doc_ids):
    tokens, width = x_query.shape
    heads = width // HD
    half = heads // 2
    zs = n_ctx // (XS * CORES)
    flat16 = pltpu.VMEM((tokens, width), BF16)
    flat32 = pltpu.VMEM((tokens, width), F32)
    square = pltpu.VMEM((tokens, tokens), F32)
    thin = pltpu.VMEM((tokens, HD), F32)
    state = lambda *lead: pltpu.VMEM((*lead, HD, HD), F32)
    dma = pltpu.SemaphoreType.DMA
    n_gain = 1 + 2 * (XS - 1) + min(zs, 4)
    vmem = pl.BlockSpec(memory_space=pltpu.VMEM)
    anywhere = pl.BlockSpec(memory_space=pl.ANY)
    big = pltpu.VMEM((tokens, width), BF16)
    outs = pl.pallas_call(
        functools.partial(kernel, n_ctx, n_head, heads),
        out_shape=(big, big, big, big, big, pltpu.VMEM((heads, HD), F32)),
        in_specs=[anywhere] * 5 + [vmem] * 2,
        out_specs=(vmem,) * 6,
        scratch_shapes=[flat16] * 5 + [flat16] * 7
        + [pltpu.VMEM((heads, tokens, tokens), BF16)] + [flat32] * 8
        + [pltpu.VMEM((heads, HD), F32), thin, square, pltpu.VMEM((2, tokens, HD), F32), thin, thin]
        + [
            state(heads), state(2, half), state(2, 2 * half), state(2, half), state(2, 2, half), state(2, half),
            pltpu.VMEM((2, heads, HD, HD), BF16),
            pltpu.VMEM((7, 8, HD), F32),
            pltpu.VMEM((n_head, 8, tokens), F32),
            pltpu.VMEM((4 + n_gain, heads, HD), F32),
            dma((5,)), dma((2, 2 * half)), dma((2, 2 * half)), dma((2, 2, half)), dma((2, 2, half)),
            dma((5,)), dma((5,)), dma((n_head - 1,)), dma((n_head - 1,)), dma((n_gain,)), dma((n_gain,)),
            dma((2, half)), dma((2, half)), pltpu.SemaphoreType.REGULAR,
        ],
        compiler_params=pltpu.CompilerParams(
            collective_id=0, has_side_effects=True, vmem_limit_bytes=56 << 20
        ),
        cost_estimate=pl.CostEstimate(flops=1 << 30, bytes_accessed=5 << 20, transcendentals=1 << 20),
    )(x_query, x_key, x_value, gate_logits, out_grad, norm_gain, doc_ids.reshape(1, tokens))
    outs = write_out([pltpu.with_memory_space_constraint(a, pltpu.VMEM) for a in outs])
    return (*outs[:5], outs[5].reshape(width))


def solution(mesh):
    n_ctx, n_head = mesh.shape["ctx"], mesh.shape["head"]
    placed = (
        P("ctx", "head"), P("ctx", "head"), P("ctx", "head"), P("ctx", "head"),
        P("head"), P("ctx", "head"), P("ctx"),
    )
    return jax.shard_map(
        functools.partial(local, n_ctx, n_head),
        mesh=mesh,
        in_specs=placed,
        out_specs=(P("ctx", "head"),) * 5 + (P("head"),),
        check_vma=False,
    )
```

```python
import functools

import jax
import jax.numpy as jnp
from jax import lax
from jax.experimental import pallas as pl
from jax.experimental.pallas import tpu as pltpu
from jax.sharding import PartitionSpec as P

HD = 128
EPS = 1e-06
MESH = pl.DeviceIdType.MESH
F32 = jnp.float32
BF16 = jnp.bfloat16
XS, CORES = 4, 2
VIA_NEXT = 2


def mm(a, b, ca, cb):
    return lax.dot_general(a, b, (((ca,), (cb,)), ((), ())), preferred_element_type=F32)


def sigmoid(x):
    return 0.5 + 0.5 * jnp.tanh(0.5 * x)


def kernel(
    n_ctx, n_head, heads,
    xq_hbm, xk_hbm, xv_hbm, gl_hbm, og_hbm, gain_ref, doc_ref,
    attn_ref, qg_ref, kg_ref, vg_ref, gg_ref, gaing_ref,
    xq, xk, xv, gl, og,
    ka, va, qa, qf, kl, vl, mg,
    wts, mix, ng, gng, sg, kp, vp, sk, sv,
    gain8, lab, mask, acc, inv_b, cc_b,
    own, sib_out, sib_in, tsend, tin, rx, st,
    meta, stat, gbuf,
    in_sem, sib_s, sib_r, far_s, far_r, meta_s, meta_r, stat_s, stat_r, gain_s, gain_r, rel_s, rel_r, token,
):
    half = heads // 2
    features = heads * HD * n_head
    c, y = lax.axis_index("ctx"), lax.axis_index("head")
    p = lax.rem(c, 2)
    g = c // 2
    chips = n_ctx // 2
    zs = n_ctx // (XS * CORES)
    z, x = c // (XS * CORES), lax.rem(g, XS)
    sibling = (g * 2 + 1 - p, y)

    def chip(d):
        return ((g + d) * 2 + p, y)

    def exists(chip_index):
        return (chip_index >= 0) & (chip_index < chips)

    def in_row(d):
        return z * XS + lax.rem(x + d + XS, XS)

    def at_z(other_z):
        return ((other_z * XS + x) * 2 + p, y)

    def when(cond, act):
        pl.when(cond)(act)

    y_peers = [(c, lax.rem(y + d, n_head)) for d in range(1, n_head)]
    row_peers = [(in_row(d) * 2 + q, y) for d in range(1, XS) for q in (p, 1 - p)]
    quad = min(zs, 4)
    quad_peers = [at_z(z // quad * quad + lax.rem(z + d, quad)) for d in range(1, quad)]
    z_peers = [at_z(lax.rem(z + d, zs)) for d in range(1, zs)]
    lead = (z == 2) | (z == 4)
    near = [chip(k) for k in (1, 2, -1, -2)]
    near_ok = [exists(g + k) for k in (1, 2, -1, -2)]
    always = [sibling] + y_peers + row_peers[1::2] + quad_peers
    chain = [(chip(k), exists(g + k)) for k in (1, 2, 3, -1, -2, -3)]
    across = at_z(jnp.where(z < quad, 4, 2))

    loads = []
    for i, (src, dst) in enumerate(((xk_hbm, xk), (xv_hbm, xv), (xq_hbm, xq), (gl_hbm, gl), (og_hbm, og))):
        cp = pltpu.make_async_copy(src, dst, in_sem.at[i])
        cp.start()
        loads.append(cp)
    barrier = pltpu.get_barrier_semaphore()
    greeted = jnp.int32(len(always))
    for q in always:
        pl.semaphore_signal(barrier, inc=1, device_id=q, device_id_type=MESH)
    for q, there in chain + ([(across, lead)] if zs > quad else []):
        when(there, lambda q=q: pl.semaphore_signal(barrier, inc=1, device_id=q, device_id_type=MESH))
        greeted = greeted + there.astype(jnp.int32)

    def remote(src, dst, ssem, rsem, dev):
        return pltpu.make_async_remote_copy(
            src_ref=src, dst_ref=dst, send_sem=ssem, recv_sem=rsem, device_id=dev, device_id_type=MESH
        )

    def loop(n, body):
        lax.fori_loop(0, n, lambda i, carry: (body(i), carry)[1], 0)

    def cols(h):
        return pl.ds(pl.multiple_of(h * HD, HD), HD)

    row = doc_ref[...].astype(F32)
    tokens = row.shape[1]
    lab[...] = jnp.broadcast_to(row, (HD, tokens)).T
    first, last = lab[0:1, :], lab[tokens - 1 : tokens, :]
    meta[0] = jnp.zeros(meta.shape[1:], F32)
    meta[2] = jnp.zeros(meta.shape[1:], F32)
    stat[0] = jnp.zeros(stat.shape[1:], F32)
    meta[0, 0:1, :] = first
    meta[0, 1:2, :] = last

    def own_part(h):
        s = cols(h)
        k = xk[:, s].astype(F32)
        v = xv[:, s].astype(F32)
        kb = (k * sigmoid(k)).astype(BF16)
        vb = (v * sigmoid(v)).astype(BF16)
        ka[:, s] = kb
        va[:, s] = vb
        in_last = lab[...] == lab[tokens - 1 : tokens, :]
        kb = jnp.where(in_last, kb.astype(F32), 0.0).astype(BF16)
        kl[:, s] = kb
        own[h] = mm(kb, vb, 0, 0)

    def sib_copy(d, i, src):
        return remote(src, sib_in.at[d, i], sib_s.at[d, i], sib_r.at[d, i], sibling)

    def ok(d, k):
        return exists(g + k * (1 - 2 * d))

    def next_copy(d, i):
        return remote(tsend.at[d, i], tin.at[d, 0, i], far_s.at[d, 0, i], far_r.at[d, 0, i], chip(1 - 2 * d))

    def pass_copy(d, i):
        return remote(tin.at[d, 0, i], tin.at[d, 1, i], far_s.at[d, 1, i], far_r.at[d, 1, i], chip(1 - 2 * d))

    def back_copy(d, i):
        return remote(tsend.at[d, i], rx.at[d, i], rel_s.at[d, i], rel_r.at[d, i], (in_row(2 * d - 1) * 2 + p, y))

    def relay_target(d):
        return in_row(1 - 2 * d) + 2 * (1 - 2 * d)

    def relay_copy(d, i):
        return remote(rx.at[d, i], tin.at[d, 1, i], far_s.at[d, 1, i], far_r.at[d, 1, i], (relay_target(d) * 2 + p, y))

    def pass_on(d, i):
        when(ok(d, -1), lambda: next_copy(d, i).wait_recv())
        when(ok(d, -1) & ok(d, 1), lambda: pass_copy(d, i).start())

    def relay(d, i):
        def act():
            back_copy(d, i).wait_recv()
            relay_copy(d, i).start()

        when(exists(relay_target(d)), act)

    def meta_copy(k):
        if k == 0:
            return remote(meta.at[0], meta.at[1], meta_s.at[0], meta_r.at[0], sibling)
        return remote(meta.at[2], meta.at[2 + k], meta_s.at[k], meta_r.at[k], near[k - 1])

    loads[0].wait()
    loads[1].wait()
    mine = p * half
    other = (1 - p) * half
    own_part(other)
    pl.semaphore_wait(barrier, greeted)
    if zs > quad:
        when(lead, lambda: pl.semaphore_signal(token, inc=1, device_id=across, device_id_type=MESH))
    meta_copy(0).start()
    sib_copy(0, 0, own.at[other]).start()

    def send_own(i):
        own_part(other + i + 1)
        sib_copy(0, i + 1, own.at[other + i + 1]).start()

    loop(half - 1, send_own)

    own_part(mine)
    meta_copy(0).wait_recv()
    lo = p == 0
    f_lo = jnp.where(lo, meta[0, 0:1, :], meta[1, 0:1, :])
    l_lo = jnp.where(lo, meta[0, 1:2, :], meta[1, 1:2, :])
    f_hi = jnp.where(lo, meta[1, 0:1, :], meta[0, 0:1, :])
    l_hi = jnp.where(lo, meta[1, 1:2, :], meta[0, 1:2, :])
    meta[2, 0:1, :] = f_lo
    meta[2, 1:2, :] = l_hi
    for k in range(1, 5):
        when(near_ok[k - 1], lambda k=k: meta_copy(k).start())

    def send_total(i, d):
        a, b = own[mine + i], sib_in[d, i]
        lo_part, hi_part = jnp.where(lo, a, b), jnp.where(lo, b, a)
        if d == 0:
            total = hi_part + jnp.where(l_lo == l_hi, lo_part, 0.0)
        else:
            total = lo_part + jnp.where(f_lo == f_hi, hi_part, 0.0)
        tsend[d, i] = total
        when(ok(d, 1), lambda: next_copy(d, i).start())
        when(ok(d, 2) & (i >= VIA_NEXT), lambda: back_copy(d, i).start())

    def fwd_total(i):
        @pl.when(i > 0)
        def _():
            own_part(mine + i)

        sib_copy(0, i, own.at[other + i]).wait_recv()
        send_total(i, 0)

    loop(half, fwd_total)

    if zs > quad:
        def spread():
            pl.semaphore_wait(token, 1)
            for q in quad_peers:
                pl.semaphore_signal(token, inc=1, device_id=q, device_id_type=MESH)

        when(lead, spread)

    t_iota = lax.broadcasted_iota(jnp.int32, (tokens, tokens), 0)
    s_iota = lax.broadcasted_iota(jnp.int32, (tokens, tokens), 1)
    lab2 = jnp.concatenate([lab[...]] * (tokens // HD), axis=1)
    mask[...] = jnp.where((lab2 == row) & (t_iota >= s_iota), 1.0, 0.0)
    gain8[...] = gain_ref[...].astype(F32).reshape(heads, HD)
    loads[2].wait()
    loads[3].wait()
    loads[4].wait()

    def inside(h):
        s = cols(h)
        q = xq[:, s].astype(F32)
        qb = (q * sigmoid(q)).astype(BF16)
        qa[:, s] = qb
        in_first = lab[...] == lab[0:1, :]
        qf[:, s] = jnp.where(in_first, qb.astype(F32), 0.0).astype(BF16)
        w = (mm(qb, ka[:, s], 1, 1) * mask[...]).astype(BF16)
        wts[h] = w
        mix[:, s] = mm(w, va[:, s], 1, 0)
        gate = sigmoid(gl[:, s].astype(F32))
        sg[:, s] = gate
        grad = og[:, s].astype(F32) * gate
        ng[:, s] = grad
        gng[:, s] = grad * gain8[pl.ds(h, 1), :]
        v = xv[:, s].astype(F32)
        gv = sigmoid(v)
        sv[:, s] = gv * (1.0 + v * (1.0 - gv))
        k = xk[:, s].astype(F32)
        gk = sigmoid(k)
        sk[:, s] = gk * (1.0 + k * (1.0 - gk))
        in_last = lab[...] == lab[tokens - 1 : tokens, :]
        vl[:, s] = jnp.where(in_last, va[:, s].astype(F32), 0.0).astype(BF16)

    turns = [lambda i=i: pass_on(0, i) for i in range(VIA_NEXT)] + [lambda i=i: relay(0, i) for i in range(VIA_NEXT, half)]
    split = heads - half // 2 - 1
    loop(split, inside)
    for j in range(half):
        turns[j]()
        if split + j < heads:
            inside(split + j)
    acc[...] = jnp.zeros_like(acc)

    for k, (back, slot) in enumerate(((2, 3), (3, 4), (0, 5), (1, 6))):
        when(near_ok[back], lambda k=k: meta_copy(k + 1).wait_recv())

        def missing(slot=slot):
            meta[slot] = jnp.full(meta.shape[1:], -1.0, F32)

        when(jnp.logical_not(near_ok[back]), missing)

    def receive(d, i, finish):
        when(ok(d, -1) & (i >= VIA_NEXT), lambda: next_copy(d, i).wait_recv())
        when(ok(d, -2), lambda: relay_copy(d, i).wait_recv())
        a, b = own[mine + i], sib_in[d, i]
        lo_part, hi_part = jnp.where(lo, a, b), jnp.where(lo, b, a)
        if d == 0:
            one, two = meta[3, 1:2, :] == f_lo, meta[4, 1:2, :] == f_lo
            edge = jnp.where(one, tin[d, 0, i], 0.0) + jnp.where(two, tin[d, 1, i], 0.0)
            inner = jnp.where(l_lo == f_hi, lo_part, 0.0) + jnp.where(f_lo == f_hi, edge, 0.0)
            to_lo, to_hi = edge, inner
        else:
            one, two = meta[5, 0:1, :] == l_hi, meta[6, 0:1, :] == l_hi
            edge = jnp.where(one, tin[d, 0, i], 0.0) + jnp.where(two, tin[d, 1, i], 0.0)
            inner = jnp.where(f_hi == l_lo, hi_part, 0.0) + jnp.where(l_hi == l_lo, edge, 0.0)
            to_lo, to_hi = inner, edge
        sib_out[d, i] = jnp.where(lo, to_hi, to_lo)
        sib_copy(d, half + i, sib_out.at[d, i]).start()
        st[d, mine + i] = jnp.where(lo, to_lo, to_hi).astype(BF16)
        finish(mine + i)

    def receive_sib(d, i, finish):
        sib_copy(d, half + i, sib_out.at[d, i]).wait_recv()
        st[d, other + i] = sib_in[d, half + i].astype(BF16)
        finish(other + i)

    def mixture(h):
        s = cols(h)
        m = mix[:, s] + mm(qf[:, s], st[0, h], 1, 0)
        mix[:, s] = m
        acc[0] += m * m
        acc[1] += gng[:, s] * m

    loop(half, lambda i: receive(0, i, mixture))
    loop(half, lambda i: receive_sib(0, i, mixture))

    stat[0, 0:1, :] = jnp.sum(acc[0].T, axis=0, keepdims=True)
    stat[0, 1:2, :] = jnp.sum(acc[1].T, axis=0, keepdims=True)

    def stat_copy(k):
        return remote(stat.at[0], stat.at[1 + k], stat_s.at[k], stat_r.at[k], y_peers[k])

    for k in range(n_head - 1):
        stat_copy(k).start()
    for k in range(n_head - 1):
        stat_copy(k).wait_recv()
    rows = stat[0]
    for k in range(n_head - 1):
        rows = rows + stat[1 + k]
    inv = lax.rsqrt(rows[0:1, :] / features + EPS)
    cc = rows[1:2, :] * (inv * inv * inv) / features
    inv_b[...] = jnp.broadcast_to(inv, (HD, tokens)).T
    cc_b[...] = jnp.broadcast_to(cc, (HD, tokens)).T

    def gain_copy(slot, dst, k, dev):
        return remote(gbuf.at[slot], gbuf.at[dst], gain_s.at[k], gain_r.at[k], dev)

    stages, k = [], 0
    for partners in ([sibling] + row_peers, z_peers):
        stages.append([gain_copy(len(stages), 2 + k + j, k + j, q) for j, q in enumerate(partners)])
        k += len(partners)

    def gain_stage(n):
        total, first_slot = gbuf[n], 2 + sum(len(st_) for st_ in stages[:n])
        for j, cp in enumerate(stages[n]):
            cp.wait_recv()
            total = total + gbuf[first_slot + j]
        if n == 1:
            gaing_ref[...] = total
            return
        gbuf[n + 1] = total
        if zs > quad:
            when(jnp.logical_not(lead), lambda: pl.semaphore_wait(token, 1))
        for cp in stages[n + 1]:
            cp.start()

    def gain_row(h):
        s = cols(h)
        gbuf[0, pl.ds(h, 1), :] = jnp.sum(ng[:, s] * mix[:, s] * inv_b[...], axis=0, keepdims=True)

    loop(heads, gain_row)
    for cp in stages[0]:
        cp.start()

    def grad_part(h):
        s = cols(h)
        m = (gng[:, s] * inv_b[...] - mix[:, s] * cc_b[...]).astype(BF16)
        mg[:, s] = m
        own[h] = mm(qf[:, s], m, 0, 0)

    for i in range(half):
        sib_copy(0, i, own.at[other + i]).wait_send()

    def send_grad(i):
        grad_part(other + i)
        sib_copy(1, i, own.at[other + i]).start()

    loop(half, send_grad)

    def bwd_total(i):
        grad_part(mine + i)
        sib_copy(1, i, own.at[other + i]).wait_recv()
        send_total(i, 1)

    loop(half, bwd_total)

    def tail(h):
        s = cols(h)
        normed = mix[:, s] * inv_b[...] * gain8[pl.ds(h, 1), :]
        gate = sg[:, s]
        attn_ref[:, s] = (normed * gate).astype(BF16)
        gg_ref[:, s] = (ng[:, s] * normed * (1.0 - gate)).astype(BF16)

    loop(heads, tail)

    def pair(h):
        s = cols(h)
        m = mg[:, s]
        w = wts[h]
        pg = (mm(m, va[:, s], 1, 1) * mask[...]).astype(BF16)
        vp[:, s] = mm(w, m, 0, 0)
        kp[:, s] = mm(pg, qa[:, s], 0, 0)
        q = xq[:, s].astype(F32)
        gq = sigmoid(q)
        slope = gq * (1.0 + q * (1.0 - gq))
        in_first = lab[...] == lab[0:1, :]
        part = mm(pg, ka[:, s], 1, 0) + jnp.where(in_first, mm(m, st[0, h], 1, 1), 0.0)
        qg_ref[:, s] = (part * slope).astype(BF16)

    turns = [lambda i=i: relay(1, i) for i in range(VIA_NEXT, half)] + [lambda i=i: pass_on(1, i) for i in range(VIA_NEXT)]
    loop(2, pair)
    gain_stage(0)
    loop(half - 2, lambda i: pair(2 + i))
    turns[0]()
    for j in range(1, half):
        pair(half + j - 1)
        turns[j]()
    pair(heads - 1)

    def final(h):
        s = cols(h)
        gb = st[1, h]
        kg_ref[:, s] = ((kp[:, s] + mm(vl[:, s], gb, 1, 1)) * sk[:, s]).astype(BF16)
        vg_ref[:, s] = ((vp[:, s] + mm(kl[:, s], gb, 1, 0)) * sv[:, s]).astype(BF16)

    loop(half, lambda i: receive(1, i, final))
    loop(half, lambda i: receive_sib(1, i, final))
    gain_stage(1)

    meta_copy(0).wait_send()
    for k in range(1, 5):
        when(near_ok[k - 1], lambda k=k: meta_copy(k).wait_send())
    for k in range(n_head - 1):
        stat_copy(k).wait_send()
    for stage in stages:
        for cp in stage:
            cp.wait_send()

    def drain(i):
        sib_copy(1, i, own.at[other + i]).wait_send()
        for d in (0, 1):
            sib_copy(d, half + i, sib_out.at[d, i]).wait_send()
            when(ok(d, 1), lambda d=d: next_copy(d, i).wait_send())
            when(ok(d, 1) & ok(d, -1) & (i < VIA_NEXT), lambda d=d: pass_copy(d, i).wait_send())

            def relayed(d=d):
                relay_copy(d, i).wait_send()

            when(ok(d, 2) & (i >= VIA_NEXT), lambda d=d: back_copy(d, i).wait_send())
            when(exists(relay_target(d)) & (i >= VIA_NEXT), relayed)

    loop(half, drain)


def write_kernel(n, *refs):
    sems = refs[-1]
    copies = [pltpu.make_async_copy(refs[i], refs[n + i], sems.at[i]) for i in range(n)]
    for cp in copies:
        cp.start()
    for cp in copies:
        cp.wait()


def write_out(arrays):
    n = len(arrays)
    return pl.pallas_call(
        functools.partial(write_kernel, n),
        out_shape=tuple(jax.ShapeDtypeStruct(a.shape, a.dtype) for a in arrays),
        in_specs=[pl.BlockSpec(memory_space=pltpu.VMEM)] * n,
        out_specs=(pl.BlockSpec(memory_space=pl.ANY),) * n,
        scratch_shapes=[pltpu.SemaphoreType.DMA((n,))],
    )(*arrays)


def local(n_ctx, n_head, x_query, x_key, x_value, gate_logits, norm_gain, out_grad, doc_ids):
    tokens, width = x_query.shape
    heads = width // HD
    half = heads // 2
    zs = n_ctx // (XS * CORES)
    flat16 = pltpu.VMEM((tokens, width), BF16)
    flat32 = pltpu.VMEM((tokens, width), F32)
    square = pltpu.VMEM((tokens, tokens), F32)
    thin = pltpu.VMEM((tokens, HD), F32)
    state = lambda *lead: pltpu.VMEM((*lead, HD, HD), F32)
    dma = pltpu.SemaphoreType.DMA
    n_gain = 1 + 2 * (XS - 1) + zs - 1
    vmem = pl.BlockSpec(memory_space=pltpu.VMEM)
    anywhere = pl.BlockSpec(memory_space=pl.ANY)
    big = pltpu.VMEM((tokens, width), BF16)
    outs = pl.pallas_call(
        functools.partial(kernel, n_ctx, n_head, heads),
        out_shape=(big, big, big, big, big, pltpu.VMEM((heads, HD), F32)),
        in_specs=[anywhere] * 5 + [vmem] * 2,
        out_specs=(vmem,) * 6,
        scratch_shapes=[flat16] * 5 + [flat16] * 7
        + [pltpu.VMEM((heads, tokens, tokens), BF16)] + [flat32] * 8
        + [pltpu.VMEM((heads, HD), F32), thin, square, pltpu.VMEM((2, tokens, HD), F32), thin, thin]
        + [
            state(heads), state(2, half), state(2, 2 * half), state(2, half), state(2, 2, half), state(2, half),
            pltpu.VMEM((2, heads, HD, HD), BF16),
            pltpu.VMEM((7, 8, HD), F32),
            pltpu.VMEM((n_head, 8, tokens), F32),
            pltpu.VMEM((2 + n_gain, heads, HD), F32),
            dma((5,)), dma((2, 2 * half)), dma((2, 2 * half)), dma((2, 2, half)), dma((2, 2, half)),
            dma((5,)), dma((5,)), dma((n_head - 1,)), dma((n_head - 1,)), dma((n_gain,)), dma((n_gain,)),
            dma((2, half)), dma((2, half)), pltpu.SemaphoreType.REGULAR,
        ],
        compiler_params=pltpu.CompilerParams(
            collective_id=0, has_side_effects=True, vmem_limit_bytes=56 << 20
        ),
        cost_estimate=pl.CostEstimate(flops=1 << 30, bytes_accessed=5 << 20, transcendentals=1 << 20),
    )(x_query, x_key, x_value, gate_logits, out_grad, norm_gain, doc_ids.reshape(1, tokens))
    outs = write_out([pltpu.with_memory_space_constraint(a, pltpu.VMEM) for a in outs])
    return (*outs[:5], outs[5].reshape(width))


def solution(mesh):
    n_ctx, n_head = mesh.shape["ctx"], mesh.shape["head"]
    placed = (
        P("ctx", "head"), P("ctx", "head"), P("ctx", "head"), P("ctx", "head"),
        P("head"), P("ctx", "head"), P("ctx"),
    )
    return jax.shard_map(
        functools.partial(local, n_ctx, n_head),
        mesh=mesh,
        in_specs=placed,
        out_specs=(P("ctx", "head"),) * 5 + (P("head"),),
        check_vma=False,
    )
```

```python
import functools

import jax
import jax.numpy as jnp
from jax import lax
from jax.experimental import pallas as pl
from jax.experimental.pallas import tpu as pltpu
from jax.sharding import PartitionSpec as P

HD = 128
EPS = 1e-06
MESH = pl.DeviceIdType.MESH
F32 = jnp.float32
BF16 = jnp.bfloat16
XS, CORES = 4, 2
VIA_NEXT = 1


def mm(a, b, ca, cb):
    return lax.dot_general(a, b, (((ca,), (cb,)), ((), ())), preferred_element_type=F32)


def sigmoid(x):
    return 0.5 + 0.5 * jnp.tanh(0.5 * x)


def kernel(
    n_ctx, n_head, heads,
    xq_hbm, xk_hbm, xv_hbm, gl_hbm, og_hbm, gain_hbm, doc_hbm,
    attn_ref, qg_ref, kg_ref, vg_ref, gg_ref, gaing_ref,
    xq, xk, xv, gl, og,
    ka, va, qa, qf, kl, vl, mg,
    wts, mix, ng, gng, sg, kp, vp, sk, sv,
    gain16, docs, gain8, lab, mask, acc, inv_b, cc_b,
    own, sib_out, sib_in, tsend, tin, rx, st,
    meta, stat, gbuf,
    in_sem, sib_s, sib_r, far_s, far_r, meta_s, meta_r, stat_s, stat_r, gain_s, gain_r, rel_s, rel_r, token,
):
    half = heads // 2
    features = heads * HD * n_head
    c, y = lax.axis_index("ctx"), lax.axis_index("head")
    p = lax.rem(c, 2)
    g = c // 2
    chips = n_ctx // 2
    zs = n_ctx // (XS * CORES)
    z, x = c // (XS * CORES), lax.rem(g, XS)
    sibling = (g * 2 + 1 - p, y)

    def chip(d):
        return ((g + d) * 2 + p, y)

    def exists(chip_index):
        return (chip_index >= 0) & (chip_index < chips)

    def in_row(d):
        return z * XS + lax.rem(x + d + XS, XS)

    def at_z(other_z):
        return ((other_z * XS + x) * 2 + p, y)

    def when(cond, act):
        pl.when(cond)(act)

    y_peers = [(c, lax.rem(y + d, n_head)) for d in range(1, n_head)]
    row_peers = [(in_row(d) * 2 + q, y) for d in range(1, XS) for q in (p, 1 - p)]
    quad = min(zs, 4)
    quad_peers = [at_z(z // quad * quad + lax.rem(z + d, quad)) for d in range(1, quad)]
    z_peers = [at_z(lax.rem(z + d, zs)) for d in range(1, zs)]
    lead = (z == 2) | (z == 4)
    near = [chip(k) for k in (1, 2, -1, -2)]
    near_ok = [exists(g + k) for k in (1, 2, -1, -2)]
    always = [sibling] + y_peers + row_peers[1::2] + quad_peers
    chain = [(chip(k), exists(g + k)) for k in (1, 2, 3, -1, -2, -3)]
    across = at_z(jnp.where(z < quad, 4, 2))

    loads = []
    for i, (src, dst) in enumerate(
        ((doc_hbm, docs), (xk_hbm, xk), (xv_hbm, xv), (xq_hbm, xq), (gl_hbm, gl), (og_hbm, og), (gain_hbm, gain16))
    ):
        cp = pltpu.make_async_copy(src, dst, in_sem.at[i])
        cp.start()
        loads.append(cp)
    barrier = pltpu.get_barrier_semaphore()
    greeted = jnp.int32(len(always))
    for q in always:
        pl.semaphore_signal(barrier, inc=1, device_id=q, device_id_type=MESH)
    for q, there in chain + ([(across, lead)] if zs > quad else []):
        when(there, lambda q=q: pl.semaphore_signal(barrier, inc=1, device_id=q, device_id_type=MESH))
        greeted = greeted + there.astype(jnp.int32)

    def remote(src, dst, ssem, rsem, dev):
        return pltpu.make_async_remote_copy(
            src_ref=src, dst_ref=dst, send_sem=ssem, recv_sem=rsem, device_id=dev, device_id_type=MESH
        )

    def loop(n, body):
        lax.fori_loop(0, n, lambda i, carry: (body(i), carry)[1], 0)

    def cols(h):
        return pl.ds(pl.multiple_of(h * HD, HD), HD)

    loads[0].wait()
    row = docs[...].astype(F32)
    tokens = row.shape[1]
    lab[...] = jnp.broadcast_to(row, (HD, tokens)).T
    first, last = lab[0:1, :], lab[tokens - 1 : tokens, :]
    meta[0] = jnp.zeros(meta.shape[1:], F32)
    meta[2] = jnp.zeros(meta.shape[1:], F32)
    stat[0] = jnp.zeros(stat.shape[1:], F32)
    meta[0, 0:1, :] = first
    meta[0, 1:2, :] = last

    def own_part(*which):
        raw = [(xk[:, cols(h)].astype(F32), xv[:, cols(h)].astype(F32)) for h in which]
        in_last = lab[...] == lab[tokens - 1 : tokens, :]
        done = []
        for k, v in raw:
            kb = (k * sigmoid(k)).astype(BF16)
            vb = (v * sigmoid(v)).astype(BF16)
            kept = jnp.where(in_last, kb.astype(F32), 0.0).astype(BF16)
            done.append((kb, vb, kept, mm(kept, vb, 0, 0)))
        for h, (kb, vb, kept, part) in zip(which, done):
            s = cols(h)
            ka[:, s] = kb
            va[:, s] = vb
            kl[:, s] = kept
            own[h] = part

    def sib_copy(d, i, src):
        return remote(src, sib_in.at[d, i], sib_s.at[d, i], sib_r.at[d, i], sibling)

    def ok(d, k):
        return exists(g + k * (1 - 2 * d))

    def next_copy(d, i):
        return remote(tsend.at[d, i], tin.at[d, 0, i], far_s.at[d, 0, i], far_r.at[d, 0, i], chip(1 - 2 * d))

    def pass_copy(d, i):
        return remote(tin.at[d, 0, i], tin.at[d, 1, i], far_s.at[d, 1, i], far_r.at[d, 1, i], chip(1 - 2 * d))

    def back_copy(d, i):
        return remote(tsend.at[d, i], rx.at[d, i], rel_s.at[d, i], rel_r.at[d, i], (relay_of(d) * 2 + p, y))

    def relay_of(d):
        return jnp.where(x == 2 - d, g + 3 * (1 - 2 * d), in_row(2 * d - 1))

    def relay_target(d):
        return jnp.where(x == 1 + d, g - 3 * (1 - 2 * d), in_row(1 - 2 * d)) + 2 * (1 - 2 * d)

    def relay_ok(d):
        source = relay_target(d) - 2 * (1 - 2 * d)
        return exists(relay_target(d)) & exists(source)

    def relay_copy(d, i):
        return remote(rx.at[d, i], tin.at[d, 1, i], far_s.at[d, 1, i], far_r.at[d, 1, i], (relay_target(d) * 2 + p, y))

    def pass_on(d, i):
        when(ok(d, -1), lambda: next_copy(d, i).wait_recv())
        when(ok(d, -1) & ok(d, 1), lambda: pass_copy(d, i).start())

    def relay(d, i):
        def act():
            back_copy(d, i).wait_recv()
            relay_copy(d, i).start()

        when(relay_ok(d), act)

    def turn(d, j):
        first = [lambda i=i: pass_on(d, i) for i in range(VIA_NEXT)]
        then = [lambda i=i: relay(d, i) for i in range(VIA_NEXT, half)]
        edge = x == d * (XS - 1)
        when(edge, (then + first)[j])
        when(jnp.logical_not(edge), (first + then)[j])

    def meta_copy(k):
        if k == 0:
            return remote(meta.at[0], meta.at[1], meta_s.at[0], meta_r.at[0], sibling)
        return remote(meta.at[2], meta.at[2 + k], meta_s.at[k], meta_r.at[k], near[k - 1])

    loads[1].wait()
    loads[2].wait()
    mine = p * half
    other = (1 - p) * half
    own_part(other)
    pl.semaphore_wait(barrier, greeted)
    if zs > quad:
        when(lead, lambda: pl.semaphore_signal(token, inc=1, device_id=across, device_id_type=MESH))
    meta_copy(0).start()
    sib_copy(0, 0, own.at[other]).start()

    def send_own(j):
        i = 2 * j + 1
        own_part(other + i, other + i + 1)
        sib_copy(0, i, own.at[other + i]).start()
        sib_copy(0, i + 1, own.at[other + i + 1]).start()

    loop((half - 1) // 2, send_own)
    if half % 2 == 0:
        own_part(other + half - 1)
        sib_copy(0, half - 1, own.at[other + half - 1]).start()

    own_part(mine)
    meta_copy(0).wait_recv()
    lo = p == 0
    f_lo = jnp.where(lo, meta[0, 0:1, :], meta[1, 0:1, :])
    l_lo = jnp.where(lo, meta[0, 1:2, :], meta[1, 1:2, :])
    f_hi = jnp.where(lo, meta[1, 0:1, :], meta[0, 0:1, :])
    l_hi = jnp.where(lo, meta[1, 1:2, :], meta[0, 1:2, :])
    meta[2, 0:1, :] = f_lo
    meta[2, 1:2, :] = l_hi
    for k in range(1, 5):
        when(near_ok[k - 1], lambda k=k: meta_copy(k).start())

    def send_total(i, d):
        a, b = own[mine + i], sib_in[d, i]
        lo_part, hi_part = jnp.where(lo, a, b), jnp.where(lo, b, a)
        if d == 0:
            total = hi_part + jnp.where(l_lo == l_hi, lo_part, 0.0)
        else:
            total = lo_part + jnp.where(f_lo == f_hi, hi_part, 0.0)
        tsend[d, i] = total
        when(ok(d, 1), lambda: next_copy(d, i).start())
        when(ok(d, 2) & (i >= VIA_NEXT), lambda: back_copy(d, i).start())

    def fwd_total(i):
        sib_copy(0, i, own.at[other + i]).wait_recv()
        send_total(i, 0)

    fwd_total(0)

    def fwd_totals(j):
        own_part(mine + 2 * j + 1, mine + 2 * j + 2)
        fwd_total(2 * j + 1)
        fwd_total(2 * j + 2)

    loop((half - 1) // 2, fwd_totals)
    if half % 2 == 0:
        own_part(mine + half - 1)
        fwd_total(half - 1)

    if zs > quad:
        def spread():
            pl.semaphore_wait(token, 1)
            for q in quad_peers:
                pl.semaphore_signal(token, inc=1, device_id=q, device_id_type=MESH)

        when(lead, spread)

    t_iota = lax.broadcasted_iota(jnp.int32, (tokens, tokens), 0)
    s_iota = lax.broadcasted_iota(jnp.int32, (tokens, tokens), 1)
    lab2 = jnp.concatenate([lab[...]] * (tokens // HD), axis=1)
    mask[...] = jnp.where((lab2 == row) & (t_iota >= s_iota), 1.0, 0.0)
    for load in loads[3:]:
        load.wait()
    gain8[...] = gain16[...].astype(F32).reshape(heads, HD)

    def inside(h):
        s = cols(h)
        q = xq[:, s].astype(F32)
        qb = (q * sigmoid(q)).astype(BF16)
        qa[:, s] = qb
        in_first = lab[...] == lab[0:1, :]
        qf[:, s] = jnp.where(in_first, qb.astype(F32), 0.0).astype(BF16)
        w = (mm(qb, ka[:, s], 1, 1) * mask[...]).astype(BF16)
        wts[h] = w
        mix[:, s] = mm(w, va[:, s], 1, 0)
        gate = sigmoid(gl[:, s].astype(F32))
        sg[:, s] = gate
        grad = og[:, s].astype(F32) * gate
        ng[:, s] = grad
        gng[:, s] = grad * gain8[pl.ds(h, 1), :]
        v = xv[:, s].astype(F32)
        gv = sigmoid(v)
        sv[:, s] = gv * (1.0 + v * (1.0 - gv))
        k = xk[:, s].astype(F32)
        gk = sigmoid(k)
        sk[:, s] = gk * (1.0 + k * (1.0 - gk))
        in_last = lab[...] == lab[tokens - 1 : tokens, :]
        vl[:, s] = jnp.where(in_last, va[:, s].astype(F32), 0.0).astype(BF16)

    split = heads - half // 2 - 1
    loop(split, inside)
    for j in range(half):
        turn(0, j)
        if split + j < heads:
            inside(split + j)
    acc[...] = jnp.zeros_like(acc)

    for k, (back, slot) in enumerate(((2, 3), (3, 4), (0, 5), (1, 6))):
        when(near_ok[back], lambda k=k: meta_copy(k + 1).wait_recv())

        def missing(slot=slot):
            meta[slot] = jnp.full(meta.shape[1:], -1.0, F32)

        when(jnp.logical_not(near_ok[back]), missing)

    def receive(d, i, finish):
        when(ok(d, -1) & (i >= VIA_NEXT), lambda: next_copy(d, i).wait_recv())
        when(ok(d, -2), lambda: relay_copy(d, i).wait_recv())
        a, b = own[mine + i], sib_in[d, i]
        lo_part, hi_part = jnp.where(lo, a, b), jnp.where(lo, b, a)
        if d == 0:
            one, two = meta[3, 1:2, :] == f_lo, meta[4, 1:2, :] == f_lo
            edge = jnp.where(one, tin[d, 0, i], 0.0) + jnp.where(two, tin[d, 1, i], 0.0)
            inner = jnp.where(l_lo == f_hi, lo_part, 0.0) + jnp.where(f_lo == f_hi, edge, 0.0)
            to_lo, to_hi = edge, inner
        else:
            one, two = meta[5, 0:1, :] == l_hi, meta[6, 0:1, :] == l_hi
            edge = jnp.where(one, tin[d, 0, i], 0.0) + jnp.where(two, tin[d, 1, i], 0.0)
            inner = jnp.where(f_hi == l_lo, hi_part, 0.0) + jnp.where(l_hi == l_lo, edge, 0.0)
            to_lo, to_hi = inner, edge
        sib_out[d, i] = jnp.where(lo, to_hi, to_lo)
        sib_copy(d, half + i, sib_out.at[d, i]).start()
        st[d, mine + i] = jnp.where(lo, to_lo, to_hi).astype(BF16)
        finish(mine + i)

    def receive_sib(d, i, finish):
        sib_copy(d, half + i, sib_out.at[d, i]).wait_recv()
        st[d, other + i] = sib_in[d, half + i].astype(BF16)
        finish(other + i)

    def mixture(h):
        s = cols(h)
        m = mix[:, s] + mm(qf[:, s], st[0, h], 1, 0)
        mix[:, s] = m
        acc[0] += m * m
        acc[1] += gng[:, s] * m

    loop(half, lambda i: receive(0, i, mixture))
    loop(half, lambda i: receive_sib(0, i, mixture))

    stat[0, 0:1, :] = jnp.sum(acc[0].T, axis=0, keepdims=True)
    stat[0, 1:2, :] = jnp.sum(acc[1].T, axis=0, keepdims=True)

    def stat_copy(k):
        return remote(stat.at[0], stat.at[1 + k], stat_s.at[k], stat_r.at[k], y_peers[k])

    for k in range(n_head - 1):
        stat_copy(k).start()
    for k in range(n_head - 1):
        stat_copy(k).wait_recv()
    rows = stat[0]
    for k in range(n_head - 1):
        rows = rows + stat[1 + k]
    inv = lax.rsqrt(rows[0:1, :] / features + EPS)
    cc = rows[1:2, :] * (inv * inv * inv) / features
    inv_b[...] = jnp.broadcast_to(inv, (HD, tokens)).T
    cc_b[...] = jnp.broadcast_to(cc, (HD, tokens)).T

    def gain_copy(slot, dst, k, dev):
        return remote(gbuf.at[slot], gbuf.at[dst], gain_s.at[k], gain_r.at[k], dev)

    stages, k = [], 0
    for partners in ([sibling] + row_peers, z_peers):
        stages.append([gain_copy(len(stages), 2 + k + j, k + j, q) for j, q in enumerate(partners)])
        k += len(partners)

    def gain_stage(n):
        total, first_slot = gbuf[n], 2 + sum(len(st_) for st_ in stages[:n])
        for j, cp in enumerate(stages[n]):
            cp.wait_recv()
            total = total + gbuf[first_slot + j]
        if n == 1:
            gaing_ref[...] = total
            return
        gbuf[n + 1] = total
        if zs > quad:
            when(jnp.logical_not(lead), lambda: pl.semaphore_wait(token, 1))
        for cp in stages[n + 1]:
            cp.start()

    def gain_row(h):
        s = cols(h)
        gbuf[0, pl.ds(h, 1), :] = jnp.sum(ng[:, s] * mix[:, s] * inv_b[...], axis=0, keepdims=True)

    loop(heads, gain_row)
    for cp in stages[0]:
        cp.start()

    def grad_part(*which):
        inv_r, cc_r = inv_b[...], cc_b[...]
        raw = [(gng[:, cols(h)], mix[:, cols(h)], qf[:, cols(h)]) for h in which]
        done = []
        for grad, plain, queries in raw:
            m = (grad * inv_r - plain * cc_r).astype(BF16)
            done.append((m, mm(queries, m, 0, 0)))
        for h, (m, part) in zip(which, done):
            mg[:, cols(h)] = m
            own[h] = part

    for i in range(half):
        sib_copy(0, i, own.at[other + i]).wait_send()

    def send_grad(j):
        grad_part(other + 2 * j, other + 2 * j + 1)
        for i in (2 * j, 2 * j + 1):
            sib_copy(1, i, own.at[other + i]).start()

    loop(half // 2, send_grad)

    def bwd_total(j):
        grad_part(mine + 2 * j, mine + 2 * j + 1)
        for i in (2 * j, 2 * j + 1):
            sib_copy(1, i, own.at[other + i]).wait_recv()
            send_total(i, 1)

    loop(half // 2, bwd_total)

    def tail(h):
        s = cols(h)
        normed = mix[:, s] * inv_b[...] * gain8[pl.ds(h, 1), :]
        gate = sg[:, s]
        attn_ref[:, s] = (normed * gate).astype(BF16)
        gg_ref[:, s] = (ng[:, s] * normed * (1.0 - gate)).astype(BF16)

    loop(heads, tail)

    def pair(h):
        s = cols(h)
        m = mg[:, s]
        w = wts[h]
        pg = (mm(m, va[:, s], 1, 1) * mask[...]).astype(BF16)
        vp[:, s] = mm(w, m, 0, 0)
        kp[:, s] = mm(pg, qa[:, s], 0, 0)
        q = xq[:, s].astype(F32)
        gq = sigmoid(q)
        slope = gq * (1.0 + q * (1.0 - gq))
        in_first = lab[...] == lab[0:1, :]
        part = mm(pg, ka[:, s], 1, 0) + jnp.where(in_first, mm(m, st[0, h], 1, 1), 0.0)
        qg_ref[:, s] = (part * slope).astype(BF16)

    loop(2, pair)
    gain_stage(0)
    loop(half - 2, lambda i: pair(2 + i))
    turn(1, 0)
    for j in range(1, half):
        pair(half + j - 1)
        turn(1, j)
    pair(heads - 1)

    def final(h):
        s = cols(h)
        gb = st[1, h]
        kg_ref[:, s] = ((kp[:, s] + mm(vl[:, s], gb, 1, 1)) * sk[:, s]).astype(BF16)
        vg_ref[:, s] = ((vp[:, s] + mm(kl[:, s], gb, 1, 0)) * sv[:, s]).astype(BF16)

    loop(half, lambda i: receive(1, i, final))
    loop(half, lambda i: receive_sib(1, i, final))
    gain_stage(1)

    meta_copy(0).wait_send()
    for k in range(1, 5):
        when(near_ok[k - 1], lambda k=k: meta_copy(k).wait_send())
    for k in range(n_head - 1):
        stat_copy(k).wait_send()
    for stage in stages:
        for cp in stage:
            cp.wait_send()

    def drain(i):
        sib_copy(1, i, own.at[other + i]).wait_send()
        for d in (0, 1):
            sib_copy(d, half + i, sib_out.at[d, i]).wait_send()
            when(ok(d, 1), lambda d=d: next_copy(d, i).wait_send())
            when(ok(d, 1) & ok(d, -1) & (i < VIA_NEXT), lambda d=d: pass_copy(d, i).wait_send())

            def relayed(d=d):
                relay_copy(d, i).wait_send()

            when(ok(d, 2) & (i >= VIA_NEXT), lambda d=d: back_copy(d, i).wait_send())
            when(relay_ok(d) & (i >= VIA_NEXT), relayed)

    loop(half, drain)


def write_kernel(n, *refs):
    sems = refs[-1]
    copies = [pltpu.make_async_copy(refs[i], refs[n + i], sems.at[i]) for i in range(n)]
    for cp in copies:
        cp.start()
    for cp in copies:
        cp.wait()


def write_out(arrays):
    n = len(arrays)
    return pl.pallas_call(
        functools.partial(write_kernel, n),
        out_shape=tuple(jax.ShapeDtypeStruct(a.shape, a.dtype) for a in arrays),
        in_specs=[pl.BlockSpec(memory_space=pltpu.VMEM)] * n,
        out_specs=(pl.BlockSpec(memory_space=pl.ANY),) * n,
        scratch_shapes=[pltpu.SemaphoreType.DMA((n,))],
    )(*arrays)


def local(n_ctx, n_head, x_query, x_key, x_value, gate_logits, norm_gain, out_grad, doc_ids):
    tokens, width = x_query.shape
    heads = width // HD
    half = heads // 2
    zs = n_ctx // (XS * CORES)
    flat16 = pltpu.VMEM((tokens, width), BF16)
    flat32 = pltpu.VMEM((tokens, width), F32)
    square = pltpu.VMEM((tokens, tokens), F32)
    thin = pltpu.VMEM((tokens, HD), F32)
    state = lambda *lead: pltpu.VMEM((*lead, HD, HD), F32)
    dma = pltpu.SemaphoreType.DMA
    n_gain = 1 + 2 * (XS - 1) + zs - 1
    vmem = pl.BlockSpec(memory_space=pltpu.VMEM)
    anywhere = pl.BlockSpec(memory_space=pl.ANY)
    big = pltpu.VMEM((tokens, width), BF16)
    outs = pl.pallas_call(
        functools.partial(kernel, n_ctx, n_head, heads),
        out_shape=(big, big, big, big, big, pltpu.VMEM((heads, HD), F32)),
        in_specs=[anywhere] * 7,
        out_specs=(vmem,) * 6,
        scratch_shapes=[flat16] * 5 + [flat16] * 7
        + [pltpu.VMEM((heads, tokens, tokens), BF16)] + [flat32] * 8
        + [pltpu.VMEM((width,), BF16), pltpu.VMEM((1, tokens), jnp.int32), pltpu.VMEM((heads, HD), F32), thin, square, pltpu.VMEM((2, tokens, HD), F32), thin, thin]
        + [
            state(heads), state(2, half), state(2, 2 * half), state(2, half), state(2, 2, half), state(2, half),
            pltpu.VMEM((2, heads, HD, HD), BF16),
            pltpu.VMEM((7, 8, HD), F32),
            pltpu.VMEM((n_head, 8, tokens), F32),
            pltpu.VMEM((2 + n_gain, heads, HD), F32),
            dma((7,)), dma((2, 2 * half)), dma((2, 2 * half)), dma((2, 2, half)), dma((2, 2, half)),
            dma((5,)), dma((5,)), dma((n_head - 1,)), dma((n_head - 1,)), dma((n_gain,)), dma((n_gain,)),
            dma((2, half)), dma((2, half)), pltpu.SemaphoreType.REGULAR,
        ],
        compiler_params=pltpu.CompilerParams(
            collective_id=0, has_side_effects=True, vmem_limit_bytes=56 << 20
        ),
        cost_estimate=pl.CostEstimate(flops=1 << 30, bytes_accessed=5 << 20, transcendentals=1 << 20),
    )(x_query, x_key, x_value, gate_logits, out_grad, norm_gain, doc_ids.reshape(1, tokens))
    outs = write_out([pltpu.with_memory_space_constraint(a, pltpu.VMEM) for a in outs])
    return (*outs[:5], outs[5].reshape(width))


def solution(mesh):
    n_ctx, n_head = mesh.shape["ctx"], mesh.shape["head"]
    placed = (
        P("ctx", "head"), P("ctx", "head"), P("ctx", "head"), P("ctx", "head"),
        P("head"), P("ctx", "head"), P("ctx"),
    )
    return jax.shard_map(
        functools.partial(local, n_ctx, n_head),
        mesh=mesh,
        in_specs=placed,
        out_specs=(P("ctx", "head"),) * 5 + (P("head"),),
        check_vma=False,
    )
```

```python
import functools

import jax
import jax.numpy as jnp
from jax import lax
from jax.experimental import pallas as pl
from jax.experimental.pallas import tpu as pltpu
from jax.sharding import PartitionSpec as P

HD = 128
EPS = 1e-06
MESH = pl.DeviceIdType.MESH
F32 = jnp.float32
BF16 = jnp.bfloat16
XS, CORES = 4, 2
PIECES = 2
VIA_NEXT = 3
VIA_ROW = 1


def mm(a, b, ca, cb):
    return lax.dot_general(a, b, (((ca,), (cb,)), ((), ())), preferred_element_type=F32)


def sigmoid(x):
    return 0.5 + 0.5 * jnp.tanh(0.5 * x)


def kernel(
    n_ctx, n_head, heads,
    xq_hbm, xk_hbm, xv_hbm, gl_hbm, og_hbm, gain_hbm, doc_hbm,
    attn_ref, qg_ref, kg_ref, vg_ref, gg_ref, gaing_ref,
    xq, xk, xv, gl, og,
    ka, va, qa, qf, kl, vl, mg,
    wts, mix, ng, gng, sg, kp, vp, sk, sv,
    gain16, docs, gain8, lab, mask, acc, inv_b, cc_b,
    own, sib_out, sib_in, tsend, tin, rx, st,
    meta, stat, gbuf,
    in_sem, sib_s, sib_r, far_s, far_r, meta_s, meta_r, stat_s, stat_r, gain_s, gain_r, rel_s, rel_r, token,
):
    half = heads // 2
    depth = HD // PIECES
    pieces = half * PIECES
    features = heads * HD * n_head
    c, y = lax.axis_index("ctx"), lax.axis_index("head")
    p = lax.rem(c, 2)
    g = c // 2
    chips = n_ctx // 2
    zs = n_ctx // (XS * CORES)
    z, x = c // (XS * CORES), lax.rem(g, XS)
    sibling = (g * 2 + 1 - p, y)

    def chip(d):
        return ((g + d) * 2 + p, y)

    def exists(chip_index):
        return (chip_index >= 0) & (chip_index < chips)

    def in_row(d):
        return z * XS + lax.rem(x + d + XS, XS)

    def at_z(other_z):
        return ((other_z * XS + x) * 2 + p, y)

    def when(cond, act):
        pl.when(cond)(act)

    y_peers = [(c, lax.rem(y + d, n_head)) for d in range(1, n_head)]
    row_peers = [(in_row(d) * 2 + q, y) for d in range(1, XS) for q in (p, 1 - p)]
    quad = min(zs, 4)
    quad_peers = [at_z(z // quad * quad + lax.rem(z + d, quad)) for d in range(1, quad)]
    z_peers = [at_z(lax.rem(z + d, zs)) for d in range(1, zs)]
    lead = (z == 2) | (z == 4)
    near = [chip(k) for k in (1, 2, -1, -2)]
    near_ok = [exists(g + k) for k in (1, 2, -1, -2)]
    always = [sibling] + y_peers + row_peers[1::2] + quad_peers
    chain = [(chip(k), exists(g + k)) for k in (1, 2, 3, -1, -2, -3)]
    across = at_z(jnp.where(z < quad, 4, 2))

    loads = []
    for i, (src, dst) in enumerate(
        ((doc_hbm, docs), (xk_hbm, xk), (xv_hbm, xv), (xq_hbm, xq), (gl_hbm, gl), (og_hbm, og), (gain_hbm, gain16))
    ):
        cp = pltpu.make_async_copy(src, dst, in_sem.at[i])
        cp.start()
        loads.append(cp)
    barrier = pltpu.get_barrier_semaphore()
    greeted = jnp.int32(len(always))
    for q in always:
        pl.semaphore_signal(barrier, inc=1, device_id=q, device_id_type=MESH)
    for q, there in chain + ([(across, lead)] if zs > quad else []):
        when(there, lambda q=q: pl.semaphore_signal(barrier, inc=1, device_id=q, device_id_type=MESH))
        greeted = greeted + there.astype(jnp.int32)

    def remote(src, dst, ssem, rsem, dev):
        return pltpu.make_async_remote_copy(
            src_ref=src, dst_ref=dst, send_sem=ssem, recv_sem=rsem, device_id=dev, device_id_type=MESH
        )

    def loop(n, body):
        lax.fori_loop(0, n, lambda i, carry: (body(i), carry)[1], 0)

    def cols(h):
        return pl.ds(pl.multiple_of(h * HD, HD), HD)

    loads[0].wait()
    row = docs[...].astype(F32)
    tokens = row.shape[1]
    lab[...] = jnp.broadcast_to(row, (HD, tokens)).T
    first, last = lab[0:1, :], lab[tokens - 1 : tokens, :]
    meta[0] = jnp.zeros(meta.shape[1:], F32)
    meta[2] = jnp.zeros(meta.shape[1:], F32)
    stat[0] = jnp.zeros(stat.shape[1:], F32)
    meta[0, 0:1, :] = first
    meta[0, 1:2, :] = last

    def own_part(*which):
        raw = [(xk[:, cols(h)].astype(F32), xv[:, cols(h)].astype(F32)) for h in which]
        in_last = lab[...] == lab[tokens - 1 : tokens, :]
        done = []
        for k, v in raw:
            kb = (k * sigmoid(k)).astype(BF16)
            vb = (v * sigmoid(v)).astype(BF16)
            kept = jnp.where(in_last, kb.astype(F32), 0.0).astype(BF16)
            done.append((kb, vb, kept, mm(kept, vb, 0, 0)))
        for h, (kb, vb, kept, part) in zip(which, done):
            s = cols(h)
            ka[:, s] = kb
            va[:, s] = vb
            kl[:, s] = kept
            own[h] = part

    def sib_copy(d, i, src):
        return remote(src, sib_in.at[d, i], sib_s.at[d, i], sib_r.at[d, i], sibling)

    def ok(d, k):
        return exists(g + k * (1 - 2 * d))

    def next_copy(d, i):
        return remote(tsend.at[d, i], tin.at[d, 0, i], far_s.at[d, 0, i], far_r.at[d, 0, i], chip(1 - 2 * d))

    def pass_copy(d, i):
        return remote(tin.at[d, 0, i], tin.at[d, 1, i], far_s.at[d, 1, i], far_r.at[d, 1, i], chip(1 - 2 * d))

    def back_copy(d, i):
        return remote(tsend.at[d, i], rx.at[d, i], rel_s.at[d, i], rel_r.at[d, i], (relay_of(d) * 2 + p, y))

    def relay_of(d):
        return jnp.where(x == 2 - d, g + 3 * (1 - 2 * d), in_row(2 * d - 1))

    def relay_target(d):
        return jnp.where(x == 1 + d, g - 3 * (1 - 2 * d), in_row(1 - 2 * d)) + 2 * (1 - 2 * d)

    def relay_ok(d):
        source = relay_target(d) - 2 * (1 - 2 * d)
        return exists(relay_target(d)) & exists(source)

    def relay_copy(d, i):
        return remote(rx.at[d, i], tin.at[d, 1, i], far_s.at[d, 1, i], far_r.at[d, 1, i], (relay_target(d) * 2 + p, y))

    def via(here):
        return jnp.where(here, VIA_ROW, VIA_NEXT)

    def passed(d, j):
        return j < via(x == (1 - d) * (XS - 1))

    def sent_back(d, j):
        return j >= via(x == 2 - d)

    def relayed(d, j):
        return j >= via(x == 1 + d)

    def pass_on(d, i):
        when(ok(d, -1) & passed(d, i), lambda: next_copy(d, i).wait_recv())
        when(ok(d, -1) & ok(d, 1) & passed(d, i), lambda: pass_copy(d, i).start())

    def relay(d, i):
        def act():
            back_copy(d, i).wait_recv()
            relay_copy(d, i).start()

        when(relay_ok(d) & relayed(d, i), act)

    def turn(d, group, groups):
        first = [lambda j=j: pass_on(d, j) for j in range(max(VIA_ROW, VIA_NEXT))]
        then = [lambda j=j: relay(d, j) for j in range(min(VIA_ROW, VIA_NEXT), pieces)]
        mixed = first[:1]
        for j in range(max(len(first) - 1, len(then))):
            mixed += first[j + 1 : j + 2] + then[j : j + 1]
        edge = x == d * (XS - 1)

        def act(order):
            for one in order[group * len(order) // groups : (group + 1) * len(order) // groups]:
                one()

        when(edge, lambda: act(then + first))
        when(jnp.logical_not(edge), lambda: act(mixed))

    def meta_copy(k):
        if k == 0:
            return remote(meta.at[0], meta.at[1], meta_s.at[0], meta_r.at[0], sibling)
        return remote(meta.at[2], meta.at[2 + k], meta_s.at[k], meta_r.at[k], near[k - 1])

    loads[1].wait()
    loads[2].wait()
    mine = p * half
    other = (1 - p) * half
    own_part(other)
    pl.semaphore_wait(barrier, greeted)
    if zs > quad:
        when(lead, lambda: pl.semaphore_signal(token, inc=1, device_id=across, device_id_type=MESH))
    meta_copy(0).start()
    sib_copy(0, 0, own.at[other]).start()

    def send_own(j):
        i = 2 * j + 1
        own_part(other + i, other + i + 1)
        sib_copy(0, i, own.at[other + i]).start()
        sib_copy(0, i + 1, own.at[other + i + 1]).start()

    loop((half - 1) // 2, send_own)
    if half % 2 == 0:
        own_part(other + half - 1)
        sib_copy(0, half - 1, own.at[other + half - 1]).start()

    own_part(mine)
    meta_copy(0).wait_recv()
    lo = p == 0
    f_lo = jnp.where(lo, meta[0, 0:1, :], meta[1, 0:1, :])
    l_lo = jnp.where(lo, meta[0, 1:2, :], meta[1, 1:2, :])
    f_hi = jnp.where(lo, meta[1, 0:1, :], meta[0, 0:1, :])
    l_hi = jnp.where(lo, meta[1, 1:2, :], meta[0, 1:2, :])
    meta[2, 0:1, :] = f_lo
    meta[2, 1:2, :] = l_hi
    for k in range(1, 5):
        when(near_ok[k - 1], lambda k=k: meta_copy(k).start())

    def send_total(i, d):
        a, b = own[mine + i], sib_in[d, i]
        lo_part, hi_part = jnp.where(lo, a, b), jnp.where(lo, b, a)
        if d == 0:
            total = hi_part + jnp.where(l_lo == l_hi, lo_part, 0.0)
        else:
            total = lo_part + jnp.where(f_lo == f_hi, hi_part, 0.0)
        for k in range(PIECES):
            j = i * PIECES + k
            tsend[d, j] = total[k * depth : (k + 1) * depth]
            when(ok(d, 1), lambda j=j: next_copy(d, j).start())
            when(ok(d, 2) & sent_back(d, j), lambda j=j: back_copy(d, j).start())

    def fwd_total(i):
        sib_copy(0, i, own.at[other + i]).wait_recv()
        send_total(i, 0)

    fwd_total(0)

    def fwd_totals(j):
        own_part(mine + 2 * j + 1, mine + 2 * j + 2)
        fwd_total(2 * j + 1)
        fwd_total(2 * j + 2)

    loop((half - 1) // 2, fwd_totals)
    if half % 2 == 0:
        own_part(mine + half - 1)
        fwd_total(half - 1)

    if zs > quad:
        def spread():
            pl.semaphore_wait(token, 1)
            for q in quad_peers:
                pl.semaphore_signal(token, inc=1, device_id=q, device_id_type=MESH)

        when(lead, spread)

    t_iota = lax.broadcasted_iota(jnp.int32, (tokens, tokens), 0)
    s_iota = lax.broadcasted_iota(jnp.int32, (tokens, tokens), 1)
    lab2 = jnp.concatenate([lab[...]] * (tokens // HD), axis=1)
    mask[...] = jnp.where((lab2 == row) & (t_iota >= s_iota), 1.0, 0.0)
    for load in loads[3:]:
        load.wait()
    gain8[...] = gain16[...].astype(F32).reshape(heads, HD)

    def inside(h):
        s = cols(h)
        q = xq[:, s].astype(F32)
        qb = (q * sigmoid(q)).astype(BF16)
        qa[:, s] = qb
        in_first = lab[...] == lab[0:1, :]
        qf[:, s] = jnp.where(in_first, qb.astype(F32), 0.0).astype(BF16)
        w = (mm(qb, ka[:, s], 1, 1) * mask[...]).astype(BF16)
        wts[h] = w
        mix[:, s] = mm(w, va[:, s], 1, 0)
        gate = sigmoid(gl[:, s].astype(F32))
        sg[:, s] = gate
        grad = og[:, s].astype(F32) * gate
        ng[:, s] = grad
        gng[:, s] = grad * gain8[pl.ds(h, 1), :]
        v = xv[:, s].astype(F32)
        gv = sigmoid(v)
        sv[:, s] = gv * (1.0 + v * (1.0 - gv))
        k = xk[:, s].astype(F32)
        gk = sigmoid(k)
        sk[:, s] = gk * (1.0 + k * (1.0 - gk))
        in_last = lab[...] == lab[tokens - 1 : tokens, :]
        vl[:, s] = jnp.where(in_last, va[:, s].astype(F32), 0.0).astype(BF16)

    groups = half + 1
    loop(heads - half, inside)
    for group in range(groups):
        turn(0, group, groups)
        if group < half:
            inside(heads - half + group)
    acc[...] = jnp.zeros_like(acc)

    for k, (back, slot) in enumerate(((2, 3), (3, 4), (0, 5), (1, 6))):
        when(near_ok[back], lambda k=k: meta_copy(k + 1).wait_recv())

        def missing(slot=slot):
            meta[slot] = jnp.full(meta.shape[1:], -1.0, F32)

        when(jnp.logical_not(near_ok[back]), missing)

    def receive(d, i, finish):
        one, two = [], []
        for k in range(PIECES):
            j = i * PIECES + k
            when(ok(d, -1) & jnp.logical_not(passed(d, j)), lambda j=j: next_copy(d, j).wait_recv())
            when(ok(d, -2), lambda j=j: relay_copy(d, j).wait_recv())
            one.append(tin[d, 0, j])
            two.append(tin[d, 1, j])
        one, two = jnp.concatenate(one, axis=0), jnp.concatenate(two, axis=0)
        a, b = own[mine + i], sib_in[d, i]
        lo_part, hi_part = jnp.where(lo, a, b), jnp.where(lo, b, a)
        if d == 0:
            one_ok, two_ok = meta[3, 1:2, :] == f_lo, meta[4, 1:2, :] == f_lo
            edge = jnp.where(one_ok, one, 0.0) + jnp.where(two_ok, two, 0.0)
            inner = jnp.where(l_lo == f_hi, lo_part, 0.0) + jnp.where(f_lo == f_hi, edge, 0.0)
            to_lo, to_hi = edge, inner
        else:
            one_ok, two_ok = meta[5, 0:1, :] == l_hi, meta[6, 0:1, :] == l_hi
            edge = jnp.where(one_ok, one, 0.0) + jnp.where(two_ok, two, 0.0)
            inner = jnp.where(f_hi == l_lo, hi_part, 0.0) + jnp.where(l_hi == l_lo, edge, 0.0)
            to_lo, to_hi = inner, edge
        sib_out[d, i] = jnp.where(lo, to_hi, to_lo)
        sib_copy(d, half + i, sib_out.at[d, i]).start()
        st[d, mine + i] = jnp.where(lo, to_lo, to_hi).astype(BF16)
        finish(mine + i)

    def receive_sib(d, i, finish):
        sib_copy(d, half + i, sib_out.at[d, i]).wait_recv()
        st[d, other + i] = sib_in[d, half + i].astype(BF16)
        finish(other + i)

    def mixture(h):
        s = cols(h)
        m = mix[:, s] + mm(qf[:, s], st[0, h], 1, 0)
        mix[:, s] = m
        acc[0] += m * m
        acc[1] += gng[:, s] * m

    loop(half, lambda i: receive(0, i, mixture))
    loop(half, lambda i: receive_sib(0, i, mixture))

    stat[0, 0:1, :] = jnp.sum(acc[0].T, axis=0, keepdims=True)
    stat[0, 1:2, :] = jnp.sum(acc[1].T, axis=0, keepdims=True)

    def stat_copy(k):
        return remote(stat.at[0], stat.at[1 + k], stat_s.at[k], stat_r.at[k], y_peers[k])

    for k in range(n_head - 1):
        stat_copy(k).start()
    for i in range(half):
        sib_copy(0, i, own.at[other + i]).wait_send()
    for k in range(n_head - 1):
        stat_copy(k).wait_recv()
    rows = stat[0]
    for k in range(n_head - 1):
        rows = rows + stat[1 + k]
    inv = lax.rsqrt(rows[0:1, :] / features + EPS)
    cc = rows[1:2, :] * (inv * inv * inv) / features
    inv_b[...] = jnp.broadcast_to(inv, (HD, tokens)).T
    cc_b[...] = jnp.broadcast_to(cc, (HD, tokens)).T

    def gain_copy(slot, dst, k, dev):
        return remote(gbuf.at[slot], gbuf.at[dst], gain_s.at[k], gain_r.at[k], dev)

    stages, k = [], 0
    for partners in ([sibling] + row_peers, z_peers):
        stages.append([gain_copy(len(stages), 2 + k + j, k + j, q) for j, q in enumerate(partners)])
        k += len(partners)

    def gain_stage(n):
        total, first_slot = gbuf[n], 2 + sum(len(st_) for st_ in stages[:n])
        for j, cp in enumerate(stages[n]):
            cp.wait_recv()
            total = total + gbuf[first_slot + j]
        if n == 1:
            gaing_ref[...] = total
            return
        gbuf[n + 1] = total
        if zs > quad:
            when(jnp.logical_not(lead), lambda: pl.semaphore_wait(token, 1))
        for cp in stages[n + 1]:
            cp.start()

    def gain_row(h):
        s = cols(h)
        gbuf[0, pl.ds(h, 1), :] = jnp.sum(ng[:, s] * mix[:, s] * inv_b[...], axis=0, keepdims=True)

    loop(heads, gain_row)
    for cp in stages[0]:
        cp.start()

    def grad_part(*which):
        inv_r, cc_r = inv_b[...], cc_b[...]
        raw = [(gng[:, cols(h)], mix[:, cols(h)], qf[:, cols(h)]) for h in which]
        done = []
        for grad, plain, queries in raw:
            m = (grad * inv_r - plain * cc_r).astype(BF16)
            done.append((m, mm(queries, m, 0, 0)))
        for h, (m, part) in zip(which, done):
            mg[:, cols(h)] = m
            own[h] = part

    def send_grad(j):
        grad_part(other + 2 * j, other + 2 * j + 1)
        for i in (2 * j, 2 * j + 1):
            sib_copy(1, i, own.at[other + i]).start()

    loop(half // 2, send_grad)

    def bwd_total(j):
        grad_part(mine + 2 * j, mine + 2 * j + 1)
        for i in (2 * j, 2 * j + 1):
            sib_copy(1, i, own.at[other + i]).wait_recv()
            send_total(i, 1)

    loop(half // 2, bwd_total)

    def tail(h):
        s = cols(h)
        normed = mix[:, s] * inv_b[...] * gain8[pl.ds(h, 1), :]
        gate = sg[:, s]
        attn_ref[:, s] = (normed * gate).astype(BF16)
        gg_ref[:, s] = (ng[:, s] * normed * (1.0 - gate)).astype(BF16)

    loop(heads, tail)

    def pair(h):
        s = cols(h)
        m = mg[:, s]
        w = wts[h]
        pg = (mm(m, va[:, s], 1, 1) * mask[...]).astype(BF16)
        vp[:, s] = mm(w, m, 0, 0)
        kp[:, s] = mm(pg, qa[:, s], 0, 0)
        q = xq[:, s].astype(F32)
        gq = sigmoid(q)
        slope = gq * (1.0 + q * (1.0 - gq))
        in_first = lab[...] == lab[0:1, :]
        part = mm(pg, ka[:, s], 1, 0) + jnp.where(in_first, mm(m, st[0, h], 1, 1), 0.0)
        qg_ref[:, s] = (part * slope).astype(BF16)

    loop(2, pair)
    gain_stage(0)
    loop(half - 2, lambda i: pair(2 + i))
    for group in range(groups):
        turn(1, group, groups)
        if group < half:
            pair(heads - half + group)

    def final(h):
        s = cols(h)
        gb = st[1, h]
        kg_ref[:, s] = ((kp[:, s] + mm(vl[:, s], gb, 1, 1)) * sk[:, s]).astype(BF16)
        vg_ref[:, s] = ((vp[:, s] + mm(kl[:, s], gb, 1, 0)) * sv[:, s]).astype(BF16)

    def drain(d):
        def pieces_out(j):
            when(ok(d, 1), lambda: next_copy(d, j).wait_send())
            when(ok(d, 1) & ok(d, -1) & passed(d, j), lambda: pass_copy(d, j).wait_send())
            when(ok(d, 2) & sent_back(d, j), lambda: back_copy(d, j).wait_send())
            when(relay_ok(d) & relayed(d, j), lambda: relay_copy(d, j).wait_send())

        loop(pieces, pieces_out)

    drain(0)
    loop(half, lambda i: sib_copy(0, half + i, sib_out.at[0, i]).wait_send())
    loop(half, lambda i: sib_copy(1, i, own.at[other + i]).wait_send())
    meta_copy(0).wait_send()
    for k in range(1, 5):
        when(near_ok[k - 1], lambda k=k: meta_copy(k).wait_send())
    for k in range(n_head - 1):
        stat_copy(k).wait_send()
    for cp in stages[0]:
        cp.wait_send()
    loop(half - 1, lambda i: receive(1, i, final))
    drain(1)
    receive(1, half - 1, final)
    loop(half, lambda i: receive_sib(1, i, final))
    gain_stage(1)

    for cp in stages[1]:
        cp.wait_send()
    loop(half, lambda i: sib_copy(1, half + i, sib_out.at[1, i]).wait_send())


def write_kernel(n, *refs):
    sems = refs[-1]
    copies = [pltpu.make_async_copy(refs[i], refs[n + i], sems.at[i]) for i in range(n)]
    for cp in copies:
        cp.start()
    for cp in copies:
        cp.wait()


def write_out(arrays):
    n = len(arrays)
    return pl.pallas_call(
        functools.partial(write_kernel, n),
        out_shape=tuple(jax.ShapeDtypeStruct(a.shape, a.dtype) for a in arrays),
        in_specs=[pl.BlockSpec(memory_space=pltpu.VMEM)] * n,
        out_specs=(pl.BlockSpec(memory_space=pl.ANY),) * n,
        scratch_shapes=[pltpu.SemaphoreType.DMA((n,))],
    )(*arrays)


def local(n_ctx, n_head, x_query, x_key, x_value, gate_logits, norm_gain, out_grad, doc_ids):
    tokens, width = x_query.shape
    heads = width // HD
    half = heads // 2
    zs = n_ctx // (XS * CORES)
    flat16 = pltpu.VMEM((tokens, width), BF16)
    flat32 = pltpu.VMEM((tokens, width), F32)
    square = pltpu.VMEM((tokens, tokens), F32)
    thin = pltpu.VMEM((tokens, HD), F32)
    state = lambda *lead: pltpu.VMEM((*lead, HD, HD), F32)
    piece = lambda *lead: pltpu.VMEM((*lead, HD // PIECES, HD), F32)
    pieces = half * PIECES
    dma = pltpu.SemaphoreType.DMA
    n_gain = 1 + 2 * (XS - 1) + zs - 1
    vmem = pl.BlockSpec(memory_space=pltpu.VMEM)
    anywhere = pl.BlockSpec(memory_space=pl.ANY)
    big = pltpu.VMEM((tokens, width), BF16)
    outs = pl.pallas_call(
        functools.partial(kernel, n_ctx, n_head, heads),
        out_shape=(big, big, big, big, big, pltpu.VMEM((heads, HD), F32)),
        in_specs=[anywhere] * 7,
        out_specs=(vmem,) * 6,
        scratch_shapes=[flat16] * 5 + [flat16] * 7
        + [pltpu.VMEM((heads, tokens, tokens), BF16)] + [flat32] * 8
        + [pltpu.VMEM((width,), BF16), pltpu.VMEM((1, tokens), jnp.int32), pltpu.VMEM((heads, HD), F32), thin, square, pltpu.VMEM((2, tokens, HD), F32), thin, thin]
        + [
            state(heads), state(2, half), state(2, 2 * half), piece(2, pieces), piece(2, 2, pieces), piece(2, pieces),
            pltpu.VMEM((2, heads, HD, HD), BF16),
            pltpu.VMEM((7, 8, HD), F32),
            pltpu.VMEM((n_head, 8, tokens), F32),
            pltpu.VMEM((2 + n_gain, heads, HD), F32),
            dma((7,)), dma((2, 2 * half)), dma((2, 2 * half)), dma((2, 2, pieces)), dma((2, 2, pieces)),
            dma((5,)), dma((5,)), dma((n_head - 1,)), dma((n_head - 1,)), dma((n_gain,)), dma((n_gain,)),
            dma((2, pieces)), dma((2, pieces)), pltpu.SemaphoreType.REGULAR,
        ],
        compiler_params=pltpu.CompilerParams(
            collective_id=0, has_side_effects=True, vmem_limit_bytes=56 << 20
        ),
        cost_estimate=pl.CostEstimate(flops=1 << 30, bytes_accessed=5 << 20, transcendentals=1 << 20),
    )(x_query, x_key, x_value, gate_logits, out_grad, norm_gain, doc_ids.reshape(1, tokens))
    outs = write_out([pltpu.with_memory_space_constraint(a, pltpu.VMEM) for a in outs])
    return (*outs[:5], outs[5].reshape(width))


def solution(mesh):
    n_ctx, n_head = mesh.shape["ctx"], mesh.shape["head"]
    placed = (
        P("ctx", "head"), P("ctx", "head"), P("ctx", "head"), P("ctx", "head"),
        P("head"), P("ctx", "head"), P("ctx"),
    )
    return jax.shard_map(
        functools.partial(local, n_ctx, n_head),
        mesh=mesh,
        in_specs=placed,
        out_specs=(P("ctx", "head"),) * 5 + (P("head"),),
        check_vma=False,
    )
```

```python
import functools

import jax
import jax.numpy as jnp
from jax import lax
from jax.experimental import pallas as pl
from jax.experimental.pallas import tpu as pltpu
from jax.sharding import PartitionSpec as P

HD = 128
EPS = 1e-06
MESH = pl.DeviceIdType.MESH
F32 = jnp.float32
BF16 = jnp.bfloat16
XS, CORES = 4, 2
PIECES = 2
VIA_NEXT = 3
VIA_ROW = 1


def mm(a, b, ca, cb):
    return lax.dot_general(a, b, (((ca,), (cb,)), ((), ())), preferred_element_type=F32)


def sigmoid(x):
    return 0.5 + 0.5 * jnp.tanh(0.5 * x)


def kernel(
    n_ctx, n_head, heads,
    xq_hbm, xk_hbm, xv_hbm, gl_hbm, og_hbm, gain_hbm, doc_hbm,
    attn_ref, qg_ref, kg_ref, vg_ref, gg_ref, gaing_ref,
    xq, xk, xv, gl, og,
    ka, va, qa, qf, kl, vl, mg,
    wts, mix, ng, gng, sg, kp, vp, sk, sv,
    gain16, docs, gain8, lab, mask, acc, inv_b, cc_b,
    own, sib_out, sib_in, tsend, tin, rx, st,
    meta, stat, gbuf,
    in_sem, sib_s, sib_r, far_s, far_r, meta_s, meta_r, stat_s, stat_r, gain_s, gain_r, rel_s, rel_r, token,
):
    half = heads // 2
    depth = HD // PIECES
    pieces = half * PIECES
    features = heads * HD * n_head
    c, y = lax.axis_index("ctx"), lax.axis_index("head")
    p = lax.rem(c, 2)
    g = c // 2
    chips = n_ctx // 2
    zs = n_ctx // (XS * CORES)
    z, x = c // (XS * CORES), lax.rem(g, XS)
    sibling = (g * 2 + 1 - p, y)

    def chip(d):
        return ((g + d) * 2 + p, y)

    def exists(chip_index):
        return (chip_index >= 0) & (chip_index < chips)

    def in_row(d):
        return z * XS + lax.rem(x + d + XS, XS)

    def at_z(other_z):
        return ((other_z * XS + x) * 2 + p, y)

    def when(cond, act):
        pl.when(cond)(act)

    y_peers = [(c, lax.rem(y + d, n_head)) for d in range(1, n_head)]
    row_peers = [(in_row(d) * 2 + q, y) for d in range(1, XS) for q in (p, 1 - p)]
    quad = min(zs, 4)
    quad_peers = [at_z(z // quad * quad + lax.rem(z + d, quad)) for d in range(1, quad)]
    z_peers = [at_z(lax.rem(z + d, zs)) for d in range(1, zs)]
    lead = (z == 2) | (z == 4)
    near = [chip(k) for k in (1, 2, -1, -2)]
    near_ok = [exists(g + k) for k in (1, 2, -1, -2)]
    always = [sibling] + y_peers + row_peers[1::2] + quad_peers
    chain = [(chip(k), exists(g + k)) for k in (1, 2, 3, -1, -2, -3)]
    across = at_z(jnp.where(z < quad, 4, 2))

    loads = []
    for i, (src, dst) in enumerate(
        ((doc_hbm, docs), (xk_hbm, xk), (xv_hbm, xv), (xq_hbm, xq), (gl_hbm, gl), (og_hbm, og), (gain_hbm, gain16))
    ):
        cp = pltpu.make_async_copy(src, dst, in_sem.at[i])
        cp.start()
        loads.append(cp)
    barrier = pltpu.get_barrier_semaphore()
    greeted = jnp.int32(len(always))
    for q in always:
        pl.semaphore_signal(barrier, inc=1, device_id=q, device_id_type=MESH)
    for q, there in chain + ([(across, lead)] if zs > quad else []):
        when(there, lambda q=q: pl.semaphore_signal(barrier, inc=1, device_id=q, device_id_type=MESH))
        greeted = greeted + there.astype(jnp.int32)

    def remote(src, dst, ssem, rsem, dev):
        return pltpu.make_async_remote_copy(
            src_ref=src, dst_ref=dst, send_sem=ssem, recv_sem=rsem, device_id=dev, device_id_type=MESH
        )

    def loop(n, body):
        lax.fori_loop(0, n, lambda i, carry: (body(i), carry)[1], 0)

    def cols(h):
        return pl.ds(pl.multiple_of(h * HD, HD), HD)

    loads[0].wait()
    row = docs[...].astype(F32)
    tokens = row.shape[1]
    lab[...] = jnp.broadcast_to(row, (HD, tokens)).T
    first, last = lab[0:1, :], lab[tokens - 1 : tokens, :]
    meta[0] = jnp.zeros(meta.shape[1:], F32)
    meta[2] = jnp.zeros(meta.shape[1:], F32)
    stat[0] = jnp.zeros(stat.shape[1:], F32)
    meta[0, 0:1, :] = first
    meta[0, 1:2, :] = last

    def own_part(*which):
        raw = [(xk[:, cols(h)].astype(F32), xv[:, cols(h)].astype(F32)) for h in which]
        in_last = lab[...] == lab[tokens - 1 : tokens, :]
        done = []
        for k, v in raw:
            kb = (k * sigmoid(k)).astype(BF16)
            vb = (v * sigmoid(v)).astype(BF16)
            kept = jnp.where(in_last, kb.astype(F32), 0.0).astype(BF16)
            done.append((kb, vb, kept, mm(kept, vb, 0, 0)))
        for h, (kb, vb, kept, part) in zip(which, done):
            s = cols(h)
            ka[:, s] = kb
            va[:, s] = vb
            kl[:, s] = kept
            own[h] = part

    def sib_copy(d, i, src):
        return remote(src, sib_in.at[d, i], sib_s.at[d, i], sib_r.at[d, i], sibling)

    def ok(d, k):
        return exists(g + k * (1 - 2 * d))

    def next_copy(d, i):
        return remote(tsend.at[d, i], tin.at[d, 0, i], far_s.at[d, 0, i], far_r.at[d, 0, i], chip(1 - 2 * d))

    def pass_copy(d, i):
        return remote(tin.at[d, 0, i], tin.at[d, 1, i], far_s.at[d, 1, i], far_r.at[d, 1, i], chip(1 - 2 * d))

    def back_copy(d, i):
        return remote(tsend.at[d, i], rx.at[d, i], rel_s.at[d, i], rel_r.at[d, i], (relay_of(d) * 2 + p, y))

    def relay_of(d):
        return jnp.where(x == 2 - d, g + 3 * (1 - 2 * d), in_row(2 * d - 1))

    def relay_target(d):
        return jnp.where(x == 1 + d, g - 3 * (1 - 2 * d), in_row(1 - 2 * d)) + 2 * (1 - 2 * d)

    def relay_ok(d):
        source = relay_target(d) - 2 * (1 - 2 * d)
        return exists(relay_target(d)) & exists(source)

    def relay_copy(d, i):
        return remote(rx.at[d, i], tin.at[d, 1, i], far_s.at[d, 1, i], far_r.at[d, 1, i], (relay_target(d) * 2 + p, y))

    def via(here):
        return jnp.where(here, VIA_ROW, VIA_NEXT)

    def passed(d, j):
        return j < via(x == (1 - d) * (XS - 1))

    def sent_back(d, j):
        return j >= via(x == 2 - d)

    def relayed(d, j):
        return j >= via(x == 1 + d)

    def pass_on(d, i):
        when(ok(d, -1) & passed(d, i), lambda: next_copy(d, i).wait_recv())
        when(ok(d, -1) & ok(d, 1) & passed(d, i), lambda: pass_copy(d, i).start())

    def relay(d, i):
        def act():
            back_copy(d, i).wait_recv()
            relay_copy(d, i).start()

        when(relay_ok(d) & relayed(d, i), act)

    def turn(d, group, groups):
        first = [lambda j=j: pass_on(d, j) for j in range(max(VIA_ROW, VIA_NEXT))]
        then = [lambda j=j: relay(d, j) for j in range(min(VIA_ROW, VIA_NEXT), pieces)]
        mixed = first[:1]
        for j in range(max(len(first) - 1, len(then))):
            mixed += first[j + 1 : j + 2] + then[j : j + 1]
        edge = x == d * (XS - 1)

        def act(order):
            for one in order[group * len(order) // groups : (group + 1) * len(order) // groups]:
                one()

        when(edge, lambda: act(then + first))
        when(jnp.logical_not(edge), lambda: act(mixed))

    def meta_copy(k):
        if k == 0:
            return remote(meta.at[0], meta.at[1], meta_s.at[0], meta_r.at[0], sibling)
        return remote(meta.at[2], meta.at[2 + k], meta_s.at[k], meta_r.at[k], near[k - 1])

    loads[1].wait()
    loads[2].wait()
    mine = p * half
    other = (1 - p) * half
    own_part(other)
    pl.semaphore_wait(barrier, greeted)
    if zs > quad:
        when(lead, lambda: pl.semaphore_signal(token, inc=1, device_id=across, device_id_type=MESH))
    meta_copy(0).start()
    sib_copy(0, 0, own.at[other]).start()

    def send_own(j):
        i = 2 * j + 1
        own_part(other + i, other + i + 1)
        sib_copy(0, i, own.at[other + i]).start()
        sib_copy(0, i + 1, own.at[other + i + 1]).start()

    loop((half - 1) // 2, send_own)
    if half % 2 == 0:
        own_part(other + half - 1)
        sib_copy(0, half - 1, own.at[other + half - 1]).start()

    own_part(mine)
    meta_copy(0).wait_recv()
    lo = p == 0
    f_lo = jnp.where(lo, meta[0, 0:1, :], meta[1, 0:1, :])
    l_lo = jnp.where(lo, meta[0, 1:2, :], meta[1, 1:2, :])
    f_hi = jnp.where(lo, meta[1, 0:1, :], meta[0, 0:1, :])
    l_hi = jnp.where(lo, meta[1, 1:2, :], meta[0, 1:2, :])
    meta[2, 0:1, :] = f_lo
    meta[2, 1:2, :] = l_hi
    for k in range(1, 5):
        when(near_ok[k - 1], lambda k=k: meta_copy(k).start())

    def send_total(i, d):
        a, b = own[mine + i], sib_in[d, i]
        lo_part, hi_part = jnp.where(lo, a, b), jnp.where(lo, b, a)
        if d == 0:
            total = hi_part + jnp.where(l_lo == l_hi, lo_part, 0.0)
        else:
            total = lo_part + jnp.where(f_lo == f_hi, hi_part, 0.0)
        for k in range(PIECES):
            j = i * PIECES + k
            tsend[d, j] = total[k * depth : (k + 1) * depth]
            when(ok(d, 1), lambda j=j: next_copy(d, j).start())
            when(ok(d, 2) & sent_back(d, j), lambda j=j: back_copy(d, j).start())

    def fwd_total(i):
        sib_copy(0, i, own.at[other + i]).wait_recv()
        send_total(i, 0)

    fwd_total(0)

    def fwd_totals(j):
        own_part(mine + 2 * j + 1, mine + 2 * j + 2)
        fwd_total(2 * j + 1)
        fwd_total(2 * j + 2)

    loop((half - 1) // 2, fwd_totals)
    if half % 2 == 0:
        own_part(mine + half - 1)
        fwd_total(half - 1)

    if zs > quad:
        def spread():
            pl.semaphore_wait(token, 1)
            for q in quad_peers:
                pl.semaphore_signal(token, inc=1, device_id=q, device_id_type=MESH)

        when(lead, spread)

    t_iota = lax.broadcasted_iota(jnp.int32, (tokens, tokens), 0)
    s_iota = lax.broadcasted_iota(jnp.int32, (tokens, tokens), 1)
    lab2 = jnp.concatenate([lab[...]] * (tokens // HD), axis=1)
    mask[...] = jnp.where((lab2 == row) & (t_iota >= s_iota), 1.0, 0.0)
    for load in loads[3:]:
        load.wait()
    gain8[...] = gain16[...].astype(F32).reshape(heads, HD)

    def inside(h):
        s = cols(h)
        q = xq[:, s].astype(F32)
        qb = (q * sigmoid(q)).astype(BF16)
        qa[:, s] = qb
        in_first = lab[...] == lab[0:1, :]
        qf[:, s] = jnp.where(in_first, qb.astype(F32), 0.0).astype(BF16)
        w = (mm(qb, ka[:, s], 1, 1) * mask[...]).astype(BF16)
        wts[h] = w
        mix[:, s] = mm(w, va[:, s], 1, 0)
        gate = sigmoid(gl[:, s].astype(F32))
        sg[:, s] = gate
        grad = og[:, s].astype(F32) * gate
        ng[:, s] = grad
        gng[:, s] = grad * gain8[pl.ds(h, 1), :]
        v = xv[:, s].astype(F32)
        gv = sigmoid(v)
        sv[:, s] = gv * (1.0 + v * (1.0 - gv))
        k = xk[:, s].astype(F32)
        gk = sigmoid(k)
        sk[:, s] = gk * (1.0 + k * (1.0 - gk))
        in_last = lab[...] == lab[tokens - 1 : tokens, :]
        vl[:, s] = jnp.where(in_last, va[:, s].astype(F32), 0.0).astype(BF16)

    groups = half + 1
    loop(heads - half, inside)
    for group in range(groups):
        turn(0, group, groups)
        if group < half:
            inside(heads - half + group)
    acc[...] = jnp.zeros_like(acc)

    for k, (back, slot) in enumerate(((2, 3), (3, 4), (0, 5), (1, 6))):
        when(near_ok[back], lambda k=k: meta_copy(k + 1).wait_recv())

        def missing(slot=slot):
            meta[slot] = jnp.full(meta.shape[1:], -1.0, F32)

        when(jnp.logical_not(near_ok[back]), missing)

    def receive(d, i, finish):
        one, two = [], []
        for k in range(PIECES):
            j = i * PIECES + k
            when(ok(d, -1) & jnp.logical_not(passed(d, j)), lambda j=j: next_copy(d, j).wait_recv())
            when(ok(d, -2), lambda j=j: relay_copy(d, j).wait_recv())
            one.append(tin[d, 0, j])
            two.append(tin[d, 1, j])
        one, two = jnp.concatenate(one, axis=0), jnp.concatenate(two, axis=0)
        a, b = own[mine + i], sib_in[d, i]
        lo_part, hi_part = jnp.where(lo, a, b), jnp.where(lo, b, a)
        if d == 0:
            one_ok, two_ok = meta[3, 1:2, :] == f_lo, meta[4, 1:2, :] == f_lo
            edge = jnp.where(one_ok, one, 0.0) + jnp.where(two_ok, two, 0.0)
            inner = jnp.where(l_lo == f_hi, lo_part, 0.0) + jnp.where(f_lo == f_hi, edge, 0.0)
            to_lo, to_hi = edge, inner
        else:
            one_ok, two_ok = meta[5, 0:1, :] == l_hi, meta[6, 0:1, :] == l_hi
            edge = jnp.where(one_ok, one, 0.0) + jnp.where(two_ok, two, 0.0)
            inner = jnp.where(f_hi == l_lo, hi_part, 0.0) + jnp.where(l_hi == l_lo, edge, 0.0)
            to_lo, to_hi = inner, edge
        sib_out[d, i] = jnp.where(lo, to_hi, to_lo)
        sib_copy(d, half + i, sib_out.at[d, i]).start()
        st[d, mine + i] = jnp.where(lo, to_lo, to_hi).astype(BF16)
        finish(mine + i)

    def receive_sib(d, i, finish):
        sib_copy(d, half + i, sib_out.at[d, i]).wait_recv()
        st[d, other + i] = sib_in[d, half + i].astype(BF16)
        finish(other + i)

    def mixture(h):
        s = cols(h)
        m = mix[:, s] + mm(qf[:, s], st[0, h], 1, 0)
        mix[:, s] = m
        acc[0] += m * m
        acc[1] += gng[:, s] * m

    loop(half, lambda i: receive(0, i, mixture))
    loop(half, lambda i: receive_sib(0, i, mixture))

    stat[0, 0:1, :] = jnp.sum(acc[0].T, axis=0, keepdims=True)
    stat[0, 1:2, :] = jnp.sum(acc[1].T, axis=0, keepdims=True)

    def stat_copy(k):
        return remote(stat.at[0], stat.at[1 + k], stat_s.at[k], stat_r.at[k], y_peers[k])

    for k in range(n_head - 1):
        stat_copy(k).start()
    for i in range(half):
        sib_copy(0, i, own.at[other + i]).wait_send()
    for k in range(n_head - 1):
        stat_copy(k).wait_recv()
    rows = stat[0]
    for k in range(n_head - 1):
        rows = rows + stat[1 + k]
    inv = lax.rsqrt(rows[0:1, :] / features + EPS)
    cc = rows[1:2, :] * (inv * inv * inv) / features
    inv_b[...] = jnp.broadcast_to(inv, (HD, tokens)).T
    cc_b[...] = jnp.broadcast_to(cc, (HD, tokens)).T

    def gain_copy(slot, dst, k, dev):
        return remote(gbuf.at[slot], gbuf.at[dst], gain_s.at[k], gain_r.at[k], dev)

    stages, k = [], 0
    for partners in ([sibling] + row_peers, z_peers):
        stages.append([gain_copy(len(stages), 2 + k + j, k + j, q) for j, q in enumerate(partners)])
        k += len(partners)

    def gain_stage(n):
        total, first_slot = gbuf[n], 2 + sum(len(st_) for st_ in stages[:n])
        for j, cp in enumerate(stages[n]):
            cp.wait_recv()
            total = total + gbuf[first_slot + j]
        if n == 1:
            gaing_ref[...] = total
            return
        gbuf[n + 1] = total
        if zs > quad:
            when(jnp.logical_not(lead), lambda: pl.semaphore_wait(token, 1))
        for cp in stages[n + 1]:
            cp.start()

    def gain_row(h):
        s = cols(h)
        gbuf[0, pl.ds(h, 1), :] = jnp.sum(ng[:, s] * mix[:, s] * inv_b[...], axis=0, keepdims=True)


    def grad_part(*which):
        inv_r, cc_r = inv_b[...], cc_b[...]
        raw = [(gng[:, cols(h)], mix[:, cols(h)], qf[:, cols(h)]) for h in which]
        done = []
        for grad, plain, queries in raw:
            m = (grad * inv_r - plain * cc_r).astype(BF16)
            done.append((m, mm(queries, m, 0, 0)))
        for h, (m, part) in zip(which, done):
            mg[:, cols(h)] = m
            own[h] = part

    def send_grad(j):
        grad_part(other + 2 * j, other + 2 * j + 1)
        for i in (2 * j, 2 * j + 1):
            sib_copy(1, i, own.at[other + i]).start()

    loop(half // 2, send_grad)
    loop(heads, gain_row)
    for cp in stages[0]:
        cp.start()

    def bwd_total(j):
        grad_part(mine + 2 * j, mine + 2 * j + 1)
        for i in (2 * j, 2 * j + 1):
            sib_copy(1, i, own.at[other + i]).wait_recv()
            send_total(i, 1)

    loop(half // 2, bwd_total)

    def tail(h):
        s = cols(h)
        normed = mix[:, s] * inv_b[...] * gain8[pl.ds(h, 1), :]
        gate = sg[:, s]
        attn_ref[:, s] = (normed * gate).astype(BF16)
        gg_ref[:, s] = (ng[:, s] * normed * (1.0 - gate)).astype(BF16)

    loop(heads, tail)

    def pair(h):
        s = cols(h)
        m = mg[:, s]
        w = wts[h]
        pg = (mm(m, va[:, s], 1, 1) * mask[...]).astype(BF16)
        vp[:, s] = mm(w, m, 0, 0)
        kp[:, s] = mm(pg, qa[:, s], 0, 0)
        q = xq[:, s].astype(F32)
        gq = sigmoid(q)
        slope = gq * (1.0 + q * (1.0 - gq))
        in_first = lab[...] == lab[0:1, :]
        part = mm(pg, ka[:, s], 1, 0) + jnp.where(in_first, mm(m, st[0, h], 1, 1), 0.0)
        qg_ref[:, s] = (part * slope).astype(BF16)

    loop(2, pair)
    gain_stage(0)
    loop(half - 2, lambda i: pair(2 + i))
    for group in range(groups):
        turn(1, group, groups)
        if group < half:
            pair(heads - half + group)

    def final(h):
        s = cols(h)
        gb = st[1, h]
        kg_ref[:, s] = ((kp[:, s] + mm(vl[:, s], gb, 1, 1)) * sk[:, s]).astype(BF16)
        vg_ref[:, s] = ((vp[:, s] + mm(kl[:, s], gb, 1, 0)) * sv[:, s]).astype(BF16)

    def drain(d):
        def pieces_out(j):
            when(ok(d, 1), lambda: next_copy(d, j).wait_send())
            when(ok(d, 1) & ok(d, -1) & passed(d, j), lambda: pass_copy(d, j).wait_send())
            when(ok(d, 2) & sent_back(d, j), lambda: back_copy(d, j).wait_send())
            when(relay_ok(d) & relayed(d, j), lambda: relay_copy(d, j).wait_send())

        loop(pieces, pieces_out)

    drain(0)
    loop(half, lambda i: sib_copy(0, half + i, sib_out.at[0, i]).wait_send())
    loop(half, lambda i: sib_copy(1, i, own.at[other + i]).wait_send())
    meta_copy(0).wait_send()
    for k in range(1, 5):
        when(near_ok[k - 1], lambda k=k: meta_copy(k).wait_send())
    for k in range(n_head - 1):
        stat_copy(k).wait_send()
    for cp in stages[0]:
        cp.wait_send()
    loop(half - 1, lambda i: receive(1, i, final))
    drain(1)
    receive(1, half - 1, final)
    loop(half, lambda i: receive_sib(1, i, final))
    gain_stage(1)

    for cp in stages[1]:
        cp.wait_send()
    loop(half, lambda i: sib_copy(1, half + i, sib_out.at[1, i]).wait_send())


def write_kernel(n, *refs):
    sems = refs[-1]
    copies = [pltpu.make_async_copy(refs[i], refs[n + i], sems.at[i]) for i in range(n)]
    for cp in copies:
        cp.start()
    for cp in copies:
        cp.wait()


def write_out(arrays):
    n = len(arrays)
    return pl.pallas_call(
        functools.partial(write_kernel, n),
        out_shape=tuple(jax.ShapeDtypeStruct(a.shape, a.dtype) for a in arrays),
        in_specs=[pl.BlockSpec(memory_space=pltpu.VMEM)] * n,
        out_specs=(pl.BlockSpec(memory_space=pl.ANY),) * n,
        scratch_shapes=[pltpu.SemaphoreType.DMA((n,))],
    )(*arrays)


def local(n_ctx, n_head, x_query, x_key, x_value, gate_logits, norm_gain, out_grad, doc_ids):
    tokens, width = x_query.shape
    heads = width // HD
    half = heads // 2
    zs = n_ctx // (XS * CORES)
    flat16 = pltpu.VMEM((tokens, width), BF16)
    flat32 = pltpu.VMEM((tokens, width), F32)
    square = pltpu.VMEM((tokens, tokens), F32)
    thin = pltpu.VMEM((tokens, HD), F32)
    state = lambda *lead: pltpu.VMEM((*lead, HD, HD), F32)
    piece = lambda *lead: pltpu.VMEM((*lead, HD // PIECES, HD), F32)
    pieces = half * PIECES
    dma = pltpu.SemaphoreType.DMA
    n_gain = 1 + 2 * (XS - 1) + zs - 1
    vmem = pl.BlockSpec(memory_space=pltpu.VMEM)
    anywhere = pl.BlockSpec(memory_space=pl.ANY)
    big = pltpu.VMEM((tokens, width), BF16)
    outs = pl.pallas_call(
        functools.partial(kernel, n_ctx, n_head, heads),
        out_shape=(big, big, big, big, big, pltpu.VMEM((heads, HD), F32)),
        in_specs=[anywhere] * 7,
        out_specs=(vmem,) * 6,
        scratch_shapes=[flat16] * 5 + [flat16] * 7
        + [pltpu.VMEM((heads, tokens, tokens), BF16)] + [flat32] * 8
        + [pltpu.VMEM((width,), BF16), pltpu.VMEM((1, tokens), jnp.int32), pltpu.VMEM((heads, HD), F32), thin, square, pltpu.VMEM((2, tokens, HD), F32), thin, thin]
        + [
            state(heads), state(2, half), state(2, 2 * half), piece(2, pieces), piece(2, 2, pieces), piece(2, pieces),
            pltpu.VMEM((2, heads, HD, HD), BF16),
            pltpu.VMEM((7, 8, HD), F32),
            pltpu.VMEM((n_head, 8, tokens), F32),
            pltpu.VMEM((2 + n_gain, heads, HD), F32),
            dma((7,)), dma((2, 2 * half)), dma((2, 2 * half)), dma((2, 2, pieces)), dma((2, 2, pieces)),
            dma((5,)), dma((5,)), dma((n_head - 1,)), dma((n_head - 1,)), dma((n_gain,)), dma((n_gain,)),
            dma((2, pieces)), dma((2, pieces)), pltpu.SemaphoreType.REGULAR,
        ],
        compiler_params=pltpu.CompilerParams(
            collective_id=0, has_side_effects=True, vmem_limit_bytes=56 << 20
        ),
        cost_estimate=pl.CostEstimate(flops=1 << 30, bytes_accessed=5 << 20, transcendentals=1 << 20),
    )(x_query, x_key, x_value, gate_logits, out_grad, norm_gain, doc_ids.reshape(1, tokens))
    outs = write_out([pltpu.with_memory_space_constraint(a, pltpu.VMEM) for a in outs])
    return (*outs[:5], outs[5].reshape(width))


def solution(mesh):
    n_ctx, n_head = mesh.shape["ctx"], mesh.shape["head"]
    placed = (
        P("ctx", "head"), P("ctx", "head"), P("ctx", "head"), P("ctx", "head"),
        P("head"), P("ctx", "head"), P("ctx"),
    )
    return jax.shard_map(
        functools.partial(local, n_ctx, n_head),
        mesh=mesh,
        in_specs=placed,
        out_specs=(P("ctx", "head"),) * 5 + (P("head"),),
        check_vma=False,
    )
```

```python
import functools

import jax
import jax.numpy as jnp
from jax import lax
from jax.experimental import pallas as pl
from jax.experimental.pallas import tpu as pltpu
from jax.sharding import PartitionSpec as P

HD = 128
EPS = 1e-06
MESH = pl.DeviceIdType.MESH
F32 = jnp.float32
BF16 = jnp.bfloat16
XS, CORES = 4, 2
PIECES = 2
VIA_NEXT = 3
VIA_ROW = 1


def mm(a, b, ca, cb):
    return lax.dot_general(a, b, (((ca,), (cb,)), ((), ())), preferred_element_type=F32)


def sigmoid(x):
    return 0.5 + 0.5 * jnp.tanh(0.5 * x)


def kernel(
    n_ctx, n_head, heads,
    xq_hbm, xk_hbm, xv_hbm, gl_hbm, og_hbm, gain_hbm, doc_hbm,
    attn_ref, qg_ref, kg_ref, vg_ref, gg_ref, gaing_ref,
    xq, xk, xv, gl, og,
    ka, va, qa, qf, kl, vl, mg,
    wts, mix, ng, gng, sg, kp, vp, sk, sv,
    gain16, docs, gain8, lab, mask, acc, inv_b, cc_b,
    own, sib_out, sib_in, tsend, tin, rx, st,
    meta, stat, gbuf,
    in_sem, sib_s, sib_r, far_s, far_r, meta_s, meta_r, stat_s, stat_r, gain_s, gain_r, rel_s, rel_r, token,
):
    half = heads // 2
    depth = HD // PIECES
    pieces = half * PIECES
    features = heads * HD * n_head
    c, y = lax.axis_index("ctx"), lax.axis_index("head")
    p = lax.rem(c, 2)
    g = c // 2
    chips = n_ctx // 2
    zs = n_ctx // (XS * CORES)
    z, x = c // (XS * CORES), lax.rem(g, XS)
    sibling = (g * 2 + 1 - p, y)

    def chip(d):
        return ((g + d) * 2 + p, y)

    def exists(chip_index):
        return (chip_index >= 0) & (chip_index < chips)

    def in_row(d):
        return z * XS + lax.rem(x + d + XS, XS)

    def at_z(other_z):
        return ((other_z * XS + x) * 2 + p, y)

    def when(cond, act):
        pl.when(cond)(act)

    y_peers = [(c, lax.rem(y + d, n_head)) for d in range(1, n_head)]
    row_peers = [(in_row(d) * 2 + q, y) for d in range(1, XS) for q in (p, 1 - p)]
    quad = min(zs, 4)
    quad_peers = [at_z(z // quad * quad + lax.rem(z + d, quad)) for d in range(1, quad)]
    z_peers = [at_z(lax.rem(z + d, zs)) for d in range(1, zs)]
    lead = (z == 2) | (z == 4)
    near = [chip(k) for k in (1, 2, -1, -2)]
    near_ok = [exists(g + k) for k in (1, 2, -1, -2)]
    always = [sibling] + y_peers + row_peers[1::2] + quad_peers
    chain = [(chip(k), exists(g + k)) for k in (1, 2, 3, -1, -2, -3)]
    across = at_z(jnp.where(z < quad, 4, 2))

    loads = []
    for i, (src, dst) in enumerate(
        ((doc_hbm, docs), (xk_hbm, xk), (xv_hbm, xv), (xq_hbm, xq), (gl_hbm, gl), (og_hbm, og), (gain_hbm, gain16))
    ):
        loads.append(pltpu.make_async_copy(src, dst, in_sem.at[i]))
    for load in loads[:3]:
        load.start()
    barrier = pltpu.get_barrier_semaphore()
    greeted = jnp.int32(len(always))
    for q in always:
        pl.semaphore_signal(barrier, inc=1, device_id=q, device_id_type=MESH)
    for q, there in chain + ([(across, lead)] if zs > quad else []):
        when(there, lambda q=q: pl.semaphore_signal(barrier, inc=1, device_id=q, device_id_type=MESH))
        greeted = greeted + there.astype(jnp.int32)
    for load in loads[3:]:
        load.start()

    def remote(src, dst, ssem, rsem, dev):
        return pltpu.make_async_remote_copy(
            src_ref=src, dst_ref=dst, send_sem=ssem, recv_sem=rsem, device_id=dev, device_id_type=MESH
        )

    def loop(n, body):
        lax.fori_loop(0, n, lambda i, carry: (body(i), carry)[1], 0)

    def cols(h):
        return pl.ds(pl.multiple_of(h * HD, HD), HD)

    loads[0].wait()
    row = docs[...].astype(F32)
    tokens = row.shape[1]
    lab[...] = jnp.broadcast_to(row, (HD, tokens)).T
    first, last = lab[0:1, :], lab[tokens - 1 : tokens, :]
    meta[0] = jnp.zeros(meta.shape[1:], F32)
    meta[2] = jnp.zeros(meta.shape[1:], F32)
    stat[0] = jnp.zeros(stat.shape[1:], F32)
    meta[0, 0:1, :] = first
    meta[0, 1:2, :] = last

    def own_part(*which):
        raw = [(xk[:, cols(h)].astype(F32), xv[:, cols(h)].astype(F32)) for h in which]
        in_last = lab[...] == lab[tokens - 1 : tokens, :]
        done = []
        for k, v in raw:
            kb = (k * sigmoid(k)).astype(BF16)
            vb = (v * sigmoid(v)).astype(BF16)
            kept = jnp.where(in_last, kb.astype(F32), 0.0).astype(BF16)
            done.append((kb, vb, kept, mm(kept, vb, 0, 0)))
        for h, (kb, vb, kept, part) in zip(which, done):
            s = cols(h)
            ka[:, s] = kb
            va[:, s] = vb
            kl[:, s] = kept
            own[h] = part

    def sib_copy(d, i, src):
        return remote(src, sib_in.at[d, i], sib_s.at[d, i], sib_r.at[d, i], sibling)

    def ok(d, k):
        return exists(g + k * (1 - 2 * d))

    def next_copy(d, i):
        return remote(tsend.at[d, i], tin.at[d, 0, i], far_s.at[d, 0, i], far_r.at[d, 0, i], chip(1 - 2 * d))

    def pass_copy(d, i):
        return remote(tin.at[d, 0, i], tin.at[d, 1, i], far_s.at[d, 1, i], far_r.at[d, 1, i], chip(1 - 2 * d))

    def back_copy(d, i):
        return remote(tsend.at[d, i], rx.at[d, i], rel_s.at[d, i], rel_r.at[d, i], (relay_of(d) * 2 + p, y))

    def relay_of(d):
        return jnp.where(x == 2 - d, g + 3 * (1 - 2 * d), in_row(2 * d - 1))

    def relay_target(d):
        return jnp.where(x == 1 + d, g - 3 * (1 - 2 * d), in_row(1 - 2 * d)) + 2 * (1 - 2 * d)

    def relay_ok(d):
        source = relay_target(d) - 2 * (1 - 2 * d)
        return exists(relay_target(d)) & exists(source)

    def relay_copy(d, i):
        return remote(rx.at[d, i], tin.at[d, 1, i], far_s.at[d, 1, i], far_r.at[d, 1, i], (relay_target(d) * 2 + p, y))

    def via(here):
        return jnp.where(here, VIA_ROW, VIA_NEXT)

    def passed(d, j):
        return j < via(x == (1 - d) * (XS - 1))

    def sent_back(d, j):
        return j >= via(x == 2 - d)

    def relayed(d, j):
        return j >= via(x == 1 + d)

    def pass_on(d, i):
        when(ok(d, -1) & passed(d, i), lambda: next_copy(d, i).wait_recv())
        when(ok(d, -1) & ok(d, 1) & passed(d, i), lambda: pass_copy(d, i).start())

    def relay(d, i):
        def act():
            back_copy(d, i).wait_recv()
            relay_copy(d, i).start()

        when(relay_ok(d) & relayed(d, i), act)

    def turn(d, group, groups):
        first = [lambda j=j: pass_on(d, j) for j in range(max(VIA_ROW, VIA_NEXT))]
        then = [lambda j=j: relay(d, j) for j in range(min(VIA_ROW, VIA_NEXT), pieces)]
        mixed = first[:1]
        for j in range(max(len(first) - 1, len(then))):
            mixed += first[j + 1 : j + 2] + then[j : j + 1]
        edge = x == d * (XS - 1)

        def act(order):
            for one in order[group * len(order) // groups : (group + 1) * len(order) // groups]:
                one()

        when(edge, lambda: act(then + first))
        when(jnp.logical_not(edge), lambda: act(mixed))

    def meta_copy(k):
        if k == 0:
            return remote(meta.at[0], meta.at[1], meta_s.at[0], meta_r.at[0], sibling)
        return remote(meta.at[2], meta.at[2 + k], meta_s.at[k], meta_r.at[k], near[k - 1])

    loads[1].wait()
    loads[2].wait()
    mine = p * half
    other = (1 - p) * half
    own_part(other)
    pl.semaphore_wait(barrier, greeted)
    if zs > quad:
        when(lead, lambda: pl.semaphore_signal(token, inc=1, device_id=across, device_id_type=MESH))
    meta_copy(0).start()
    sib_copy(0, 0, own.at[other]).start()

    def send_own(j):
        i = 2 * j + 1
        own_part(other + i, other + i + 1)
        sib_copy(0, i, own.at[other + i]).start()
        sib_copy(0, i + 1, own.at[other + i + 1]).start()

    loop((half - 1) // 2, send_own)
    if half % 2 == 0:
        own_part(other + half - 1)
        sib_copy(0, half - 1, own.at[other + half - 1]).start()

    own_part(mine)
    meta_copy(0).wait_recv()
    lo = p == 0
    f_lo = jnp.where(lo, meta[0, 0:1, :], meta[1, 0:1, :])
    l_lo = jnp.where(lo, meta[0, 1:2, :], meta[1, 1:2, :])
    f_hi = jnp.where(lo, meta[1, 0:1, :], meta[0, 0:1, :])
    l_hi = jnp.where(lo, meta[1, 1:2, :], meta[0, 1:2, :])
    meta[2, 0:1, :] = f_lo
    meta[2, 1:2, :] = l_hi
    for k in range(1, 5):
        when(near_ok[k - 1], lambda k=k: meta_copy(k).start())

    def send_total(i, d):
        a, b = own[mine + i], sib_in[d, i]
        lo_part, hi_part = jnp.where(lo, a, b), jnp.where(lo, b, a)
        if d == 0:
            total = hi_part + jnp.where(l_lo == l_hi, lo_part, 0.0)
        else:
            total = lo_part + jnp.where(f_lo == f_hi, hi_part, 0.0)
        for k in range(PIECES):
            j = i * PIECES + k
            tsend[d, j] = total[k * depth : (k + 1) * depth]
            when(ok(d, 1), lambda j=j: next_copy(d, j).start())
            when(ok(d, 2) & sent_back(d, j), lambda j=j: back_copy(d, j).start())

    def fwd_total(i):
        sib_copy(0, i, own.at[other + i]).wait_recv()
        send_total(i, 0)

    fwd_total(0)

    def fwd_totals(j):
        own_part(mine + 2 * j + 1, mine + 2 * j + 2)
        fwd_total(2 * j + 1)
        fwd_total(2 * j + 2)

    loop((half - 1) // 2, fwd_totals)
    if half % 2 == 0:
        own_part(mine + half - 1)
        fwd_total(half - 1)

    if zs > quad:
        def spread():
            pl.semaphore_wait(token, 1)
            for q in quad_peers:
                pl.semaphore_signal(token, inc=1, device_id=q, device_id_type=MESH)

        when(lead, spread)

    t_iota = lax.broadcasted_iota(jnp.int32, (tokens, tokens), 0)
    s_iota = lax.broadcasted_iota(jnp.int32, (tokens, tokens), 1)
    lab2 = jnp.concatenate([lab[...]] * (tokens // HD), axis=1)
    mask[...] = jnp.where((lab2 == row) & (t_iota >= s_iota), 1.0, 0.0)
    for load in loads[3:]:
        load.wait()
    gain8[...] = gain16[...].astype(F32).reshape(heads, HD)

    def inside(h):
        s = cols(h)
        q = xq[:, s].astype(F32)
        qb = (q * sigmoid(q)).astype(BF16)
        qa[:, s] = qb
        in_first = lab[...] == lab[0:1, :]
        qf[:, s] = jnp.where(in_first, qb.astype(F32), 0.0).astype(BF16)
        w = (mm(qb, ka[:, s], 1, 1) * mask[...]).astype(BF16)
        wts[h] = w
        mix[:, s] = mm(w, va[:, s], 1, 0)
        gate = sigmoid(gl[:, s].astype(F32))
        sg[:, s] = gate
        grad = og[:, s].astype(F32) * gate
        ng[:, s] = grad
        gng[:, s] = grad * gain8[pl.ds(h, 1), :]
        v = xv[:, s].astype(F32)
        gv = sigmoid(v)
        sv[:, s] = gv * (1.0 + v * (1.0 - gv))
        k = xk[:, s].astype(F32)
        gk = sigmoid(k)
        sk[:, s] = gk * (1.0 + k * (1.0 - gk))
        in_last = lab[...] == lab[tokens - 1 : tokens, :]
        vl[:, s] = jnp.where(in_last, va[:, s].astype(F32), 0.0).astype(BF16)

    groups = half + 1
    loop(heads - half, inside)
    for group in range(groups):
        turn(0, group, groups)
        if group < half:
            inside(heads - half + group)
    acc[...] = jnp.zeros_like(acc)

    for k, (back, slot) in enumerate(((2, 3), (3, 4), (0, 5), (1, 6))):
        when(near_ok[back], lambda k=k: meta_copy(k + 1).wait_recv())

        def missing(slot=slot):
            meta[slot] = jnp.full(meta.shape[1:], -1.0, F32)

        when(jnp.logical_not(near_ok[back]), missing)

    def receive(d, i, finish):
        one, two = [], []
        for k in range(PIECES):
            j = i * PIECES + k
            when(ok(d, -1) & jnp.logical_not(passed(d, j)), lambda j=j: next_copy(d, j).wait_recv())
            when(ok(d, -2), lambda j=j: relay_copy(d, j).wait_recv())
            one.append(tin[d, 0, j])
            two.append(tin[d, 1, j])
        one, two = jnp.concatenate(one, axis=0), jnp.concatenate(two, axis=0)
        a, b = own[mine + i], sib_in[d, i]
        lo_part, hi_part = jnp.where(lo, a, b), jnp.where(lo, b, a)
        if d == 0:
            one_ok, two_ok = meta[3, 1:2, :] == f_lo, meta[4, 1:2, :] == f_lo
            edge = jnp.where(one_ok, one, 0.0) + jnp.where(two_ok, two, 0.0)
            inner = jnp.where(l_lo == f_hi, lo_part, 0.0) + jnp.where(f_lo == f_hi, edge, 0.0)
            to_lo, to_hi = edge, inner
        else:
            one_ok, two_ok = meta[5, 0:1, :] == l_hi, meta[6, 0:1, :] == l_hi
            edge = jnp.where(one_ok, one, 0.0) + jnp.where(two_ok, two, 0.0)
            inner = jnp.where(f_hi == l_lo, hi_part, 0.0) + jnp.where(l_hi == l_lo, edge, 0.0)
            to_lo, to_hi = inner, edge
        sib_out[d, i] = jnp.where(lo, to_hi, to_lo)
        sib_copy(d, half + i, sib_out.at[d, i]).start()
        st[d, mine + i] = jnp.where(lo, to_lo, to_hi).astype(BF16)
        finish(mine + i)

    def receive_sib(d, i, finish):
        sib_copy(d, half + i, sib_out.at[d, i]).wait_recv()
        st[d, other + i] = sib_in[d, half + i].astype(BF16)
        finish(other + i)

    def mixture(h):
        s = cols(h)
        m = mix[:, s] + mm(qf[:, s], st[0, h], 1, 0)
        mix[:, s] = m
        acc[0] += m * m
        acc[1] += gng[:, s] * m

    loop(half, lambda i: receive(0, i, mixture))
    loop(half, lambda i: receive_sib(0, i, mixture))

    stat[0, 0:1, :] = jnp.sum(acc[0].T, axis=0, keepdims=True)
    stat[0, 1:2, :] = jnp.sum(acc[1].T, axis=0, keepdims=True)

    def stat_copy(k):
        return remote(stat.at[0], stat.at[1 + k], stat_s.at[k], stat_r.at[k], y_peers[k])

    for k in range(n_head - 1):
        stat_copy(k).start()
    for i in range(half):
        sib_copy(0, i, own.at[other + i]).wait_send()
    for k in range(n_head - 1):
        stat_copy(k).wait_recv()
    rows = stat[0]
    for k in range(n_head - 1):
        rows = rows + stat[1 + k]
    inv = lax.rsqrt(rows[0:1, :] / features + EPS)
    cc = rows[1:2, :] * (inv * inv * inv) / features
    inv_b[...] = jnp.broadcast_to(inv, (HD, tokens)).T
    cc_b[...] = jnp.broadcast_to(cc, (HD, tokens)).T

    def gain_copy(slot, dst, k, dev):
        return remote(gbuf.at[slot], gbuf.at[dst], gain_s.at[k], gain_r.at[k], dev)

    stages, k = [], 0
    for partners in ([sibling] + row_peers, z_peers):
        stages.append([gain_copy(len(stages), 2 + k + j, k + j, q) for j, q in enumerate(partners)])
        k += len(partners)

    def gain_stage(n):
        total, first_slot = gbuf[n], 2 + sum(len(st_) for st_ in stages[:n])
        for j, cp in enumerate(stages[n]):
            cp.wait_recv()
            total = total + gbuf[first_slot + j]
        if n == 1:
            gaing_ref[...] = total
            return
        gbuf[n + 1] = total
        if zs > quad:
            when(jnp.logical_not(lead), lambda: pl.semaphore_wait(token, 1))
        for cp in stages[n + 1]:
            cp.start()

    def gain_row(h):
        s = cols(h)
        gbuf[0, pl.ds(h, 1), :] = jnp.sum(ng[:, s] * mix[:, s] * inv_b[...], axis=0, keepdims=True)


    def grad_part(*which):
        inv_r, cc_r = inv_b[...], cc_b[...]
        raw = [(gng[:, cols(h)], mix[:, cols(h)], qf[:, cols(h)]) for h in which]
        done = []
        for grad, plain, queries in raw:
            m = (grad * inv_r - plain * cc_r).astype(BF16)
            done.append((m, mm(queries, m, 0, 0)))
        for h, (m, part) in zip(which, done):
            mg[:, cols(h)] = m
            own[h] = part

    def send_grad(j):
        grad_part(other + 2 * j, other + 2 * j + 1)
        for i in (2 * j, 2 * j + 1):
            sib_copy(1, i, own.at[other + i]).start()

    loop(half // 2, send_grad)
    loop(heads, gain_row)
    for cp in stages[0]:
        cp.start()

    def bwd_total(j):
        grad_part(mine + 2 * j, mine + 2 * j + 1)
        for i in (2 * j, 2 * j + 1):
            sib_copy(1, i, own.at[other + i]).wait_recv()
            send_total(i, 1)

    loop(half // 2, bwd_total)

    def tail(h):
        s = cols(h)
        normed = mix[:, s] * inv_b[...] * gain8[pl.ds(h, 1), :]
        gate = sg[:, s]
        attn_ref[:, s] = (normed * gate).astype(BF16)
        gg_ref[:, s] = (ng[:, s] * normed * (1.0 - gate)).astype(BF16)

    loop(heads, tail)

    def pair(h):
        s = cols(h)
        m = mg[:, s]
        w = wts[h]
        pg = (mm(m, va[:, s], 1, 1) * mask[...]).astype(BF16)
        vp[:, s] = mm(w, m, 0, 0)
        kp[:, s] = mm(pg, qa[:, s], 0, 0)
        q = xq[:, s].astype(F32)
        gq = sigmoid(q)
        slope = gq * (1.0 + q * (1.0 - gq))
        in_first = lab[...] == lab[0:1, :]
        part = mm(pg, ka[:, s], 1, 0) + jnp.where(in_first, mm(m, st[0, h], 1, 1), 0.0)
        qg_ref[:, s] = (part * slope).astype(BF16)

    loop(2, pair)
    gain_stage(0)
    loop(half - 2, lambda i: pair(2 + i))
    for group in range(groups):
        turn(1, group, groups)
        if group < half:
            pair(heads - half + group)

    def final(h):
        s = cols(h)
        gb = st[1, h]
        kg_ref[:, s] = ((kp[:, s] + mm(vl[:, s], gb, 1, 1)) * sk[:, s]).astype(BF16)
        vg_ref[:, s] = ((vp[:, s] + mm(kl[:, s], gb, 1, 0)) * sv[:, s]).astype(BF16)

    def drain(d):
        def pieces_out(j):
            when(ok(d, 1), lambda: next_copy(d, j).wait_send())
            when(ok(d, 1) & ok(d, -1) & passed(d, j), lambda: pass_copy(d, j).wait_send())
            when(ok(d, 2) & sent_back(d, j), lambda: back_copy(d, j).wait_send())
            when(relay_ok(d) & relayed(d, j), lambda: relay_copy(d, j).wait_send())

        loop(pieces, pieces_out)

    drain(0)
    loop(half, lambda i: sib_copy(0, half + i, sib_out.at[0, i]).wait_send())
    loop(half, lambda i: sib_copy(1, i, own.at[other + i]).wait_send())
    meta_copy(0).wait_send()
    for k in range(1, 5):
        when(near_ok[k - 1], lambda k=k: meta_copy(k).wait_send())
    for k in range(n_head - 1):
        stat_copy(k).wait_send()
    for cp in stages[0]:
        cp.wait_send()
    loop(half - 1, lambda i: receive(1, i, final))
    drain(1)
    receive(1, half - 1, final)
    loop(half, lambda i: receive_sib(1, i, final))
    gain_stage(1)

    for cp in stages[1]:
        cp.wait_send()
    loop(half, lambda i: sib_copy(1, half + i, sib_out.at[1, i]).wait_send())


def write_kernel(n, *refs):
    sems = refs[-1]
    copies = [pltpu.make_async_copy(refs[i], refs[n + i], sems.at[i]) for i in range(n)]
    for cp in copies:
        cp.start()
    for cp in copies:
        cp.wait()


def write_out(arrays):
    n = len(arrays)
    return pl.pallas_call(
        functools.partial(write_kernel, n),
        out_shape=tuple(jax.ShapeDtypeStruct(a.shape, a.dtype) for a in arrays),
        in_specs=[pl.BlockSpec(memory_space=pltpu.VMEM)] * n,
        out_specs=(pl.BlockSpec(memory_space=pl.ANY),) * n,
        scratch_shapes=[pltpu.SemaphoreType.DMA((n,))],
    )(*arrays)


def local(n_ctx, n_head, x_query, x_key, x_value, gate_logits, norm_gain, out_grad, doc_ids):
    tokens, width = x_query.shape
    heads = width // HD
    half = heads // 2
    zs = n_ctx // (XS * CORES)
    flat16 = pltpu.VMEM((tokens, width), BF16)
    flat32 = pltpu.VMEM((tokens, width), F32)
    square = pltpu.VMEM((tokens, tokens), F32)
    thin = pltpu.VMEM((tokens, HD), F32)
    state = lambda *lead: pltpu.VMEM((*lead, HD, HD), F32)
    piece = lambda *lead: pltpu.VMEM((*lead, HD // PIECES, HD), F32)
    pieces = half * PIECES
    dma = pltpu.SemaphoreType.DMA
    n_gain = 1 + 2 * (XS - 1) + zs - 1
    vmem = pl.BlockSpec(memory_space=pltpu.VMEM)
    anywhere = pl.BlockSpec(memory_space=pl.ANY)
    big = pltpu.VMEM((tokens, width), BF16)
    outs = pl.pallas_call(
        functools.partial(kernel, n_ctx, n_head, heads),
        out_shape=(big, big, big, big, big, pltpu.VMEM((heads, HD), F32)),
        in_specs=[anywhere] * 7,
        out_specs=(vmem,) * 6,
        scratch_shapes=[flat16] * 5 + [flat16] * 7
        + [pltpu.VMEM((heads, tokens, tokens), BF16)] + [flat32] * 8
        + [pltpu.VMEM((width,), BF16), pltpu.VMEM((1, tokens), jnp.int32), pltpu.VMEM((heads, HD), F32), thin, square, pltpu.VMEM((2, tokens, HD), F32), thin, thin]
        + [
            state(heads), state(2, half), state(2, 2 * half), piece(2, pieces), piece(2, 2, pieces), piece(2, pieces),
            pltpu.VMEM((2, heads, HD, HD), BF16),
            pltpu.VMEM((7, 8, HD), F32),
            pltpu.VMEM((n_head, 8, tokens), F32),
            pltpu.VMEM((2 + n_gain, heads, HD), F32),
            dma((7,)), dma((2, 2 * half)), dma((2, 2 * half)), dma((2, 2, pieces)), dma((2, 2, pieces)),
            dma((5,)), dma((5,)), dma((n_head - 1,)), dma((n_head - 1,)), dma((n_gain,)), dma((n_gain,)),
            dma((2, pieces)), dma((2, pieces)), pltpu.SemaphoreType.REGULAR,
        ],
        compiler_params=pltpu.CompilerParams(
            collective_id=0, has_side_effects=True, vmem_limit_bytes=56 << 20
        ),
        cost_estimate=pl.CostEstimate(flops=1 << 30, bytes_accessed=5 << 20, transcendentals=1 << 20),
    )(x_query, x_key, x_value, gate_logits, out_grad, norm_gain, doc_ids.reshape(1, tokens))
    outs = write_out([pltpu.with_memory_space_constraint(a, pltpu.VMEM) for a in outs])
    return (*outs[:5], outs[5].reshape(width))


def solution(mesh):
    n_ctx, n_head = mesh.shape["ctx"], mesh.shape["head"]
    placed = (
        P("ctx", "head"), P("ctx", "head"), P("ctx", "head"), P("ctx", "head"),
        P("head"), P("ctx", "head"), P("ctx"),
    )
    return jax.shard_map(
        functools.partial(local, n_ctx, n_head),
        mesh=mesh,
        in_specs=placed,
        out_specs=(P("ctx", "head"),) * 5 + (P("head"),),
        check_vma=False,
    )
```
